128 devices in a mesh: ctx: 16 (over y, z), exp: 8 (over x, core).
Axes of the slice: x: 4, y: 4, z: 4, core: 2. Of those that a mesh axis runs over, the one named last changes fastest.
Arguments:
- span_q: bfloat16 [1024, 5120], P('ctx', 'exp'), may hold values from -12 to 12
- decode_q: bfloat16 [1024, 5120], P('ctx', 'exp'), may hold values from -12 to 12
- k_cache: bfloat16 [49152, 1024], P('ctx', 'exp'), may hold values from -12 to 12
- v_cache: bfloat16 [49152, 1024], P('ctx', 'exp'), may hold values from -6 to 6
- span_k: bfloat16 [1024, 1024], P('ctx', 'exp'), may hold values from -6 to 6
- span_v: bfloat16 [1024, 1024], P('ctx', 'exp'), may hold values from -6 to 6
- decode_k: bfloat16 [1024, 1024], P('ctx', 'exp'), may hold values from -6 to 6
- decode_v: bfloat16 [1024, 1024], P('ctx', 'exp'), may hold values from -6 to 6
- decode_pos: int32 [1024], replicated, may hold values from 2 to 49152
- out_weight: bfloat16 [5120, 5120], P('exp'), may hold values from -0.078125 to 0.078125
- span_resid: bfloat16 [1024, 5120], P(('ctx', 'exp')), may hold values from -3 to 3
- decode_resid: bfloat16 [1024, 5120], P(('ctx', 'exp')), may hold values from -3 to 3
- norm_gain: bfloat16 [5120], replicated, may hold values from 0.099609375 to 1.8984375
- router: bfloat16 [5120, 8], replicated, may hold values from -0.15625 to 0.15625
- span_expert: int32 [1024, 1], P(('ctx', 'exp')), may hold values from 0 to 7; in each aligned block of 8 rows (0 to 7, 8 to 15, ...) at most 2 rows name the same one
- decode_expert: int32 [1024, 1], P(('ctx', 'exp')), may hold values from 0 to 7; in each aligned block of 8 rows (0 to 7, 8 to 15, ...) at most 2 rows name the same one
- w_gate: bfloat16 [8, 5120, 8192], P('exp', None, 'ctx'), may hold values from -0.078125 to 0.078125
- w_up: bfloat16 [8, 5120, 8192], P('exp', None, 'ctx'), may hold values from -0.078125 to 0.078125
- w_down: bfloat16 [8, 8192, 5120], P('exp', 'ctx'), may hold values from -0.0625 to 0.0625
Outputs:
- span_out: bfloat16 [1024, 5120], P(('ctx', 'exp'))
- decode_out: bfloat16 [1024, 5120], P(('ctx', 'exp'))
The draws below stay inside these ranges and needn't reach their ends.
Inputs may be any that keep to these rules, and one draw needn't show every extreme that they name: `span_expert`: among the rows of one device, no expert is chosen by more than 2 rows. `decode_expert`: among the rows of one device, no expert is chosen by more than 2 rows.
All inputs are finite; a program needn't handle non-finite values.
Results may differ from the reference program's by a relative error of at most 0.015.
Values may be sent and summed in bfloat16 or wider, within the bound.
A program may use at most 192 MiB of HBM per device.

```python
import math
import jax
import jax.numpy as jnp
import numpy as np
from jax import lax

D = 5120
HEADS = 40
KV_HEADS = 8
HEAD = 128
FF = 8192
TOK_DEV = 64
PRE_DEV = 3072
SPAN = 1024
DECODE = 1024
PREFIX = 49152
EXPERTS = 8
CAP = 2
N_CTX = 16
N_EXP = 8


def shared_direction(key):
    signs = jax.random.bernoulli(jax.random.fold_in(key, 50), 0.5, (HEAD,))
    return jnp.where(signs, 2.4, -2.4).astype(jnp.float32)


def shared_own(key):
    base = jax.random.normal(jax.random.fold_in(key, 60), (DECODE, KV_HEADS, HEAD), jnp.float32)
    return jnp.clip(base, -4.0, 4.0)


def plant_rows(key, values, direction, repeats):
    picked_rows = jax.random.randint(key, (8,), 0, values.shape[0])
    strength = jax.random.uniform(jax.random.fold_in(key, 1), (8,), jnp.float32, 3.0, 5.0)
    planted = strength[:, None] * jnp.tile(direction, repeats)[None, :]
    return values.at[picked_rows].set(planted)


def draw_span_q(key, part):
    direction = shared_direction(key)
    key = jax.random.fold_in(key, 1)
    values = jnp.clip(3.0 * jax.random.normal(key, (SPAN, HEADS * HEAD), jnp.float32), -12.0, 12.0)
    values = plant_rows(jax.random.fold_in(key, 9), values, direction, HEADS)
    return values.astype(jnp.bfloat16)


def draw_decode_q(key, part):
    direction = shared_direction(key)
    common = shared_own(key)
    key = jax.random.fold_in(key, 2)
    group = HEADS // KV_HEADS
    noise = jax.random.normal(key, (DECODE, KV_HEADS, group, HEAD), jnp.float32)
    values = 3.0 * (0.6 * common[:, :, None, :] + 0.8 * noise)
    values = jnp.clip(values, -12.0, 12.0).reshape(DECODE, HEADS * HEAD)
    values = plant_rows(jax.random.fold_in(key, 9), values, direction, HEADS)
    return values.astype(jnp.bfloat16)


def draw_decode_k(key, part):
    common = shared_own(key)
    values = jnp.clip(0.6 * common, -6.0, 6.0).reshape(DECODE, KV_HEADS * HEAD)
    return values.astype(jnp.bfloat16)


def draw_k_cache(key, part):
    direction = shared_direction(key)
    key = jax.random.fold_in(key, 3)
    values = jnp.clip(jax.random.normal(key, (PREFIX, KV_HEADS * HEAD), jnp.float32), -6.0, 6.0)
    jitter = 0.02 * jax.random.normal(jax.random.fold_in(key, 4), (2, KV_HEADS * HEAD), jnp.float32)
    leading_scale = jnp.array([1.875 - 0.1 / HEAD ** 0.5, 1.875], jnp.float32)
    leading = leading_scale[:, None] * jnp.tile(direction, KV_HEADS)[None, :] + jitter
    values = values.at[0:2].set(leading)
    return values.astype(jnp.bfloat16)


def touch_ends(values, own_key, low, high):
    longest = values.shape.index(max(values.shape))
    spots = []
    for shift in (0, 1):
        where = [jax.random.randint(jax.random.fold_in(own_key, axis), (), 0, length) for axis, length in enumerate(values.shape)]
        where[longest] = (where[longest] + shift) % values.shape[longest]
        spots.append(tuple(where))
    return values.at[spots[0]].set(low).at[spots[1]].set(high)


def level_of(rng, dims, shards, low, high):
    loudness = 1.0
    for position, blocks in shards:
        heights = jax.random.uniform(jax.random.fold_in(jax.random.fold_in(rng, 6), position), (blocks,), jnp.float32, low / len(shards), high / len(shards))
        loudness = loudness * jnp.repeat(jnp.exp(heights), dims[position] // blocks).reshape((-1,) + (1,) * (len(dims) - 1 - position))
    return loudness


def assign_block(stream_key, own, number, rows, number_of, top, bound, skew):
    order = jax.random.permutation(stream_key, number_of)
    crowded, usual = portions_of(number_of, rows * top, bound, skew, True), portions_of(number_of, rows * top, bound, skew, False)
    places = jnp.arange(number_of)

    def named(sizes, rotation):
        used = int((sizes > 0).sum())
        fixed = max(1, used // 4)
        moved = fixed + (places - fixed + rotation * (used - fixed)) % max(1, number_of - fixed)
        return jnp.zeros((number_of,), jnp.int32).at[order[jnp.where(places < fixed, places, moved)]].set(jnp.asarray(sizes, jnp.int32))

    sizes = jnp.where(number % 4 == 0, named(crowded, number // 4), named(usual, number - number // 4 - 1))
    mixed = jax.random.permutation(jax.random.fold_in(own, 3), number_of)
    donor, sink = mixed[0:number_of // 2 * 2:2], mixed[1:number_of // 2 * 2:2]
    margin = jnp.minimum(sizes[donor] - 1, bound - sizes[sink]) // 2
    margin = jnp.where((donor == order[0]) | (sink == order[0]) | (sizes[sink] == 0), 0, jnp.maximum(margin, 0))
    moved = jax.random.randint(jax.random.fold_in(own, 4), (number_of // 2,), 0, 1 << 20) % (margin + 1)
    sizes = sizes.at[donor].add(-moved).at[sink].add(moved)
    items = jnp.searchsorted(jnp.cumsum(sizes), jnp.arange(rows * top), side="right").astype(jnp.int32)
    listing = items.reshape(top, rows).T
    listing = listing[jax.random.permutation(jax.random.fold_in(own, 1), rows)]
    rotation = jax.random.randint(jax.random.fold_in(own, 2), (rows, 1), 0, top)
    return jnp.take_along_axis(listing, (jnp.arange(top)[None, :] + rotation) % top, axis=1)


def portions_of(count, total, reach, slope, full):
    portions = [(1 << 20) // math.isqrt(standing ** slope) + 1 for standing in range(1, count + 1)]
    largest = reach if full else min(reach, max(-(-total // count), total * portions[0] // sum(portions)))
    least = 1 if total - largest >= count - 1 else 0
    holding, spare = [largest] + [least] * (count - 1), total - largest - least * (count - 1)
    while spare > 0:
        movable = [i for i in range(1, count) if holding[i] < largest] or [i for i in range(1, count) if holding[i] < reach]
        pool, remaining = sum([portions[i] for i in movable]), spare
        for i in movable:
            more = min(reach - holding[i], max(1, remaining * portions[i] // pool), spare)
            holding[i] = holding[i] + more
            spare = spare - more
    return np.array(holding)


def bell_draw(own_key, extent, spread, most, pieces=(), kind=jnp.bfloat16):
    drawn = jax.random.normal(own_key, extent, jnp.float32) * spread
    if len(pieces) > 0:
        drawn = level_of(own_key, extent, pieces, -0.22, 0.18) * drawn
    return jnp.clip(drawn, min=-most, max=most).astype(kind)


def setup_inputs(seed: int = 0) -> dict:
    arg_keys = jax.random.split(jax.random.key(seed), 20)
    span_q = draw_span_q(jax.random.fold_in(arg_keys[19], 71), 0)
    decode_q = draw_decode_q(jax.random.fold_in(arg_keys[19], 71), 0)
    k_cache = draw_k_cache(jax.random.fold_in(arg_keys[19], 71), 0)
    v_cache = bell_draw(arg_keys[3], (PREFIX, KV_HEADS * HEAD), 1.0, 6.0, ((0, 16), (1, 8)))
    span_k = bell_draw(arg_keys[4], (SPAN, KV_HEADS * HEAD), 1.0, 6.0, ((0, 16), (1, 8)))
    span_v = bell_draw(arg_keys[5], (SPAN, KV_HEADS * HEAD), 1.0, 6.0, ((0, 16), (1, 8)))
    decode_k = draw_decode_k(jax.random.fold_in(arg_keys[19], 71), 0)
    decode_v = bell_draw(arg_keys[7], (DECODE, KV_HEADS * HEAD), 1.0, 6.0, ((0, 16), (1, 8)))
    decode_pos = touch_ends(jax.random.randint(arg_keys[8], (DECODE,), 2, PREFIX + 1), jax.random.fold_in(arg_keys[8], 1), 2, PREFIX).astype(jnp.int32)
    out_weight = bell_draw(arg_keys[9], (HEADS * HEAD, D), (HEADS * HEAD) ** -0.5, 0.078125, ((0, 8),))
    span_resid = bell_draw(arg_keys[10], (SPAN, D), 0.5, 3.0, ((0, 128),))
    decode_resid = bell_draw(arg_keys[11], (DECODE, D), 0.5, 3.0, ((0, 128),))
    norm_gain = jnp.clip(1.0 + 0.18 * jax.random.normal(arg_keys[12], (D,), jnp.float32), 0.099609375, 1.8984375).astype(jnp.bfloat16)
    router = bell_draw(arg_keys[13], (D, EXPERTS), (D // 4) ** -0.5, 0.15625)
    span_expert_keys = jax.random.split(jax.random.fold_in(arg_keys[14], 1), SPAN // (TOK_DEV // N_EXP))
    span_expert_turns = jax.random.permutation(jax.random.fold_in(arg_keys[14], 3), SPAN // (TOK_DEV // N_EXP))
    span_expert = jax.vmap(lambda own, number: assign_block(jax.random.fold_in(arg_keys[14], 2), own, number, TOK_DEV // N_EXP, EXPERTS, 1, CAP, 2))(span_expert_keys, span_expert_turns).reshape((SPAN, 1))
    decode_expert_keys = jax.random.split(jax.random.fold_in(arg_keys[15], 1), DECODE // (TOK_DEV // N_EXP))
    decode_expert_turns = jax.random.permutation(jax.random.fold_in(arg_keys[15], 3), DECODE // (TOK_DEV // N_EXP))
    decode_expert = jax.vmap(lambda own, number: assign_block(jax.random.fold_in(arg_keys[15], 2), own, number, TOK_DEV // N_EXP, EXPERTS, 1, CAP, 2))(decode_expert_keys, decode_expert_turns).reshape((DECODE, 1))
    w_gate = bell_draw(arg_keys[16], (EXPERTS, D, FF), D ** -0.5, 0.078125, ((0, 8), (2, 16)))
    w_up = bell_draw(arg_keys[17], (EXPERTS, D, FF), D ** -0.5, 0.078125, ((0, 8), (2, 16)))
    w_down = bell_draw(arg_keys[18], (EXPERTS, FF, D), FF ** -0.5, 0.0625, ((0, 8), (1, 16)))
    return {"span_q": span_q, "decode_q": decode_q, "k_cache": k_cache, "v_cache": v_cache, "span_k": span_k, "span_v": span_v, "decode_k": decode_k, "decode_v": decode_v, "decode_pos": decode_pos, "out_weight": out_weight, "span_resid": span_resid, "decode_resid": decode_resid, "norm_gain": norm_gain, "router": router, "span_expert": span_expert, "decode_expert": decode_expert, "w_gate": w_gate, "w_up": w_up, "w_down": w_down}


NEG = -1e+30
EPS = 1e-05

def block_part(queries, key_pre, val_pre, key_span, val_span, decode_pos, block_id):
    row_count = queries.shape[0]
    score_scale = HEAD ** (-0.5)
    prefix_pos = block_id * PRE_DEV + jnp.arange(PRE_DEV, dtype=jnp.int32)
    span_pos = block_id * TOK_DEV + jnp.arange(TOK_DEV, dtype=jnp.int32)
    row_ids = jnp.arange(row_count, dtype=jnp.int32)
    query_f = queries.astype(jnp.float32)
    score_pre = jnp.einsum('rsgd,jd->rsgj', query_f, key_pre.astype(jnp.float32)) * score_scale
    score_span = jnp.einsum('rsgd,jd->rsgj', query_f, key_span.astype(jnp.float32)) * score_scale
    seen_pre = jnp.stack([jnp.ones((row_count, PRE_DEV), bool), prefix_pos[None, :] < decode_pos[:, None]], 1)[:, :, None, :]
    seen_span = jnp.stack([span_pos[None, :] <= row_ids[:, None], jnp.zeros((row_count, TOK_DEV), bool)], 1)[:, :, None, :]
    score_pre = jnp.where(seen_pre, score_pre, NEG)
    score_span = jnp.where(seen_span, score_span, NEG)
    top_max = jnp.maximum(lax.optimization_barrier(jnp.max(score_pre, -1)), lax.optimization_barrier(jnp.max(score_span, -1)))
    weight_pre = jnp.where(seen_pre, jnp.exp(score_pre - top_max[..., None]), 0.0)
    weight_span = jnp.where(seen_span, jnp.exp(score_span - top_max[..., None]), 0.0)
    denom_part = lax.optimization_barrier(jnp.sum(weight_pre, -1)) + lax.optimization_barrier(jnp.sum(weight_span, -1))
    numer_part = jnp.einsum('rsgj,jd->rsgd', weight_pre.astype(jnp.bfloat16).astype(jnp.float32), val_pre.astype(jnp.float32))
    numer_part = numer_part + jnp.einsum('rsgj,jd->rsgd', weight_span.astype(jnp.bfloat16).astype(jnp.float32), val_span.astype(jnp.float32))
    return (top_max, numer_part, denom_part)

def run_expert(packed):
    rows_in, gate_w, up_w, down_w = packed
    gate_h = jnp.dot(rows_in, gate_w, preferred_element_type=jnp.float32)
    up_h = jnp.dot(rows_in, up_w, preferred_element_type=jnp.float32)
    hidden = (jax.nn.silu(gate_h) * up_h).astype(jnp.bfloat16)
    slots = hidden.shape[0]
    hidden_blocks = hidden.reshape(slots, N_CTX, FF // N_CTX).astype(jnp.float32)
    down_blocks = down_w.reshape(N_CTX, FF // N_CTX, D).astype(jnp.float32)
    partial_out = jnp.einsum('nch,chd->cnd', hidden_blocks, down_blocks)
    rounded = lax.optimization_barrier(partial_out.astype(jnp.bfloat16)).astype(jnp.float32)
    return lax.optimization_barrier(jnp.sum(rounded, 0)).astype(jnp.bfloat16)

def reference(span_q, decode_q, k_cache, v_cache, span_k, span_v, decode_k, decode_v, decode_pos, out_weight, span_resid, decode_resid, norm_gain, router, span_expert, decode_expert, w_gate, w_up, w_down):
    row_count = SPAN
    head_group = HEADS // KV_HEADS
    score_scale = HEAD ** (-0.5)
    queries = jnp.stack([span_q, decode_q], 1).reshape(row_count, 2, KV_HEADS, head_group, HEAD).transpose(2, 0, 1, 3, 4)
    keys_all = k_cache.reshape(PREFIX, KV_HEADS, HEAD).transpose(1, 0, 2)
    vals_all = v_cache.reshape(PREFIX, KV_HEADS, HEAD).transpose(1, 0, 2)
    span_keys = span_k.reshape(SPAN, KV_HEADS, HEAD).transpose(1, 0, 2)
    span_vals = span_v.reshape(SPAN, KV_HEADS, HEAD).transpose(1, 0, 2)
    block_ids = jnp.arange(N_CTX, dtype=jnp.int32)

    def all_heads(block_id):

        def head_part(packed):
            query_h, key_h, val_h, ckey_h, cval_h = packed
            key_pre = lax.dynamic_slice_in_dim(key_h, block_id * PRE_DEV, PRE_DEV, 0)
            val_pre = lax.dynamic_slice_in_dim(val_h, block_id * PRE_DEV, PRE_DEV, 0)
            key_span = lax.dynamic_slice_in_dim(ckey_h, block_id * TOK_DEV, TOK_DEV, 0)
            val_span = lax.dynamic_slice_in_dim(cval_h, block_id * TOK_DEV, TOK_DEV, 0)
            return block_part(query_h, key_pre, val_pre, key_span, val_span, decode_pos, block_id)
        return lax.map(head_part, (queries, keys_all, vals_all, span_keys, span_vals))
    block_tops = lax.map(lambda block_id: all_heads(block_id)[0], block_ids)
    top_all = lax.optimization_barrier(jnp.max(block_tops, 0))

    def accumulate(carry, block_id):
        top_b, numer_b, denom_b = all_heads(block_id)
        factor = jnp.exp(top_b - top_all)
        return ((carry[0] + numer_b * factor[..., None], carry[1] + denom_b * factor), None)
    start = (jnp.zeros((KV_HEADS, row_count, 2, head_group, HEAD), jnp.float32), jnp.zeros((KV_HEADS, row_count, 2, head_group), jnp.float32))
    (numer_sum, denom_sum), _ = lax.scan(accumulate, start, block_ids)
    dec_query = decode_q.reshape(row_count, KV_HEADS, head_group, HEAD).astype(jnp.float32)
    dec_key = decode_k.reshape(row_count, KV_HEADS, HEAD).astype(jnp.float32)
    own_score = lax.optimization_barrier(jnp.sum(dec_query * dec_key[:, :, None, :], -1)) * score_scale
    own_score = jnp.stack([jnp.full_like(own_score, NEG), own_score], 1).transpose(2, 0, 1, 3)
    dec_val = decode_v.reshape(row_count, KV_HEADS, HEAD).astype(jnp.float32)
    own_val = jnp.stack([jnp.zeros_like(dec_val), dec_val], 1).transpose(2, 0, 1, 3)
    total_max = jnp.maximum(top_all, own_score)
    scale_top = jnp.exp(top_all - total_max)
    own_weight = jnp.exp(own_score - total_max)
    numer = numer_sum * scale_top[..., None] + own_weight[..., None] * own_val[:, :, :, None, :]
    denom = denom_sum * scale_top + own_weight
    attn = (numer / denom[..., None]).astype(jnp.bfloat16)
    attn = attn.transpose(1, 2, 0, 3, 4).reshape(row_count * 2, HEADS * HEAD)
    residual = jnp.stack([span_resid, decode_resid], 1).reshape(row_count * 2, D).astype(jnp.float32)
    stream = jnp.dot(attn, out_weight, preferred_element_type=jnp.float32) + residual
    normed = (stream * lax.rsqrt(lax.optimization_barrier(jnp.mean(stream * stream, -1, keepdims=True)) + EPS) * norm_gain.astype(jnp.float32)).astype(jnp.bfloat16)
    logits = jnp.dot(normed, router, preferred_element_type=jnp.float32)
    expert_ids = jnp.stack([span_expert[:, 0], decode_expert[:, 0]], 1)
    flat_ids = expert_ids.reshape(-1)
    gate_value = jax.nn.sigmoid(jnp.take_along_axis(logits, flat_ids[:, None], 1)[:, 0])
    routed_in = (normed.astype(jnp.float32) * gate_value[:, None]).astype(jnp.bfloat16)
    block_total = N_CTX * N_EXP
    per_block = row_count // block_total
    blocked = expert_ids.reshape(block_total, per_block, 2)
    same_expert = blocked[:, :, None, :] == blocked[:, None, :, :]
    row_order = jnp.arange(per_block, dtype=jnp.int32)
    earlier = row_order[None, :] < row_order[:, None]
    slot_index = lax.optimization_barrier(jnp.sum(same_expert & earlier[None, :, :, None], 2)).astype(jnp.int32)
    column = (jnp.arange(block_total, dtype=jnp.int32)[:, None, None] * (2 * CAP) + jnp.arange(2, dtype=jnp.int32)[None, None, :] * CAP + slot_index).reshape(-1)
    buffer = jnp.zeros((EXPERTS, block_total * 2 * CAP, D), jnp.bfloat16).at[flat_ids, column].set(routed_in)
    expert_all = lax.map(run_expert, (buffer, w_gate, w_up, w_down))
    routed = expert_all[flat_ids, column].astype(jnp.float32)
    result = (stream + routed).astype(jnp.bfloat16).reshape(row_count, 2, D)
    return (result[:, 0], result[:, 1])
```

```python
import functools

import jax
import jax.numpy as jnp
from jax import lax
from jax.experimental import pallas as pl
from jax.experimental.pallas import tpu as pltpu
from jax.sharding import PartitionSpec as P

HEAD = 128
NEG = -1e30
EPS = 1e-05
SCALE2 = HEAD ** (-0.5) * 1.4426950408889634
NY = 4
NZ = 4
N_CTX = NY * NZ
N_X = 4
N_EXP = 2 * N_X
KEY_TILE = 512
MESH = pl.DeviceIdType.MESH
BF16 = jnp.bfloat16
F32 = jnp.float32


def copy_to(src, dst, send_sem, recv_sem, **where):
    return pltpu.make_async_remote_copy(
        src_ref=src,
        dst_ref=dst,
        send_sem=send_sem,
        recv_sem=recv_sem,
        device_id=where,
        device_id_type=MESH,
    )


def attention_kernel(
    sq_ref, dq_ref, pos_ref, k_ref, v_ref, sk_ref, sv_ref, dk_ref, dv_ref,
    attn_ref,
    qbuf, kx, vx, num_out, stat_out, num_in, stat_in,
    q_send, q_recv, n_send, n_recv, s_send, s_recv,
):
    tok = sq_ref.shape[0]
    heads = sq_ref.shape[1] // HEAD
    pre = k_ref.shape[0]
    me = lax.axis_index("ctx")
    my_y, my_z = me // NZ, me % NZ

    def offset(k):
        off = (5 * k) % N_CTX
        return off // NZ, off % NZ

    def ahead(k):
        dy, dz = offset(k)
        return ((my_y + dy) % NY) * NZ + (my_z + dz) % NZ

    def behind(k):
        dy, dz = offset(k)
        return ((my_y + NY - dy) % NY) * NZ + (my_z + NZ - dz) % NZ

    barrier = pltpu.get_barrier_semaphore()
    for k in range(1, N_CTX):
        pl.semaphore_signal(barrier, inc=1, device_id={"ctx": ahead(k)}, device_id_type=MESH)
    qbuf[me, :tok] = sq_ref[...]
    qbuf[me, tok:] = dq_ref[...]
    kx[:pre] = k_ref[...]
    kx[pre : pre + tok] = sk_ref[...]
    kx[pre + tok :] = jnp.zeros((kx.shape[0] - pre - tok, HEAD), BF16)
    vx[:pre, :HEAD] = v_ref[...]
    vx[pre : pre + tok, :HEAD] = sv_ref[...]
    vx[pre + tok :, :HEAD] = jnp.zeros((kx.shape[0] - pre - tok, HEAD), BF16)
    vx[:, HEAD:] = jnp.ones((vx.shape[0], HEAD), BF16)
    pl.semaphore_wait(barrier, N_CTX - 1)

    def q_copy(k):
        return copy_to(qbuf.at[me], qbuf.at[me], q_send.at[k], q_recv.at[k], ctx=ahead(k))

    def send_q(k, carry):
        q_copy(k).start()
        return carry

    lax.fori_loop(1, N_CTX, send_q, 0)

    def n_copy(k, dst):
        return copy_to(num_out.at[k], num_in.at[k], n_send.at[k], n_recv.at[k], ctx=dst)

    def s_copy(k, dst):
        return copy_to(stat_out.at[k], stat_in.at[k], s_send.at[k], s_recv.at[k], ctx=dst)

    def tile_step(q, lo, hi, mask, state):
        s = lax.dot_general(
            q, kx[lo:hi], (((1,), (1,)), ((), ())), preferred_element_type=F32
        )
        s = mask(s, lo)
        top = jnp.max(s, -1, keepdims=True)
        if state is not None:
            old_top, old = state
            top = jnp.maximum(old_top, top)
        w = jnp.exp2((s - top) * SCALE2).astype(BF16)
        out = jnp.dot(w, vx[lo:hi], preferred_element_type=F32)
        if state is not None:
            out = old * jnp.exp2((old_top - top) * SCALE2) + out
        return top, out

    lane = lax.broadcasted_iota(jnp.int32, (tok, HEAD), 1)

    def block(k, carry):
        src = behind(k)

        @pl.when(k > 0)
        def _():
            q_copy(k).wait_recv()

        row = lax.broadcasted_iota(jnp.int32, (tok, 1), 0)
        span_limit = src * tok + row - me * tok + 1
        span_limit = jnp.clip(span_limit, 0, tok)
        dec_limit = pos_ref[src][:, :1] - me * pre
        stats = []
        for kind in range(2):
            q = qbuf[src, kind * tok : (kind + 1) * tok]
            q = jnp.concatenate([q[:, h * HEAD : (h + 1) * HEAD] for h in range(heads)], 0)
            limit = jnp.concatenate([span_limit if kind == 0 else dec_limit] * heads, 0)

            def mask(s, lo):
                if kind == 0 and lo + s.shape[1] <= pre:
                    return s
                column = lax.broadcasted_iota(jnp.int32, s.shape, 1)
                if kind == 0:
                    hidden_from = limit + (pre - lo)
                else:
                    hidden_from = limit - lo
                return jnp.where(column < hidden_from, s, NEG)

            state = None
            last = pre + (kx.shape[0] - pre if kind == 0 else 0)
            edges = list(range(0, pre, KEY_TILE)) + [last]
            for lo, hi in zip(edges[:-1], edges[1:]):
                state = tile_step(q, lo, hi, mask, state)
            top, out = state
            num = out[:, :HEAD].astype(BF16)
            stat = jnp.zeros((tok, HEAD), F32)
            for h in range(heads):
                rows = slice(h * tok, (h + 1) * tok)
                num_out[k, kind * tok : (kind + 1) * tok, h * HEAD : (h + 1) * HEAD] = num[rows]
                stat = jnp.where(lane == h, top[rows], stat)
                stat = jnp.where(lane == 8 + h, out[rows, HEAD:], stat)
            stats.append(stat)
        stat_out[k] = jnp.concatenate(stats, 0).T[:16]

        @pl.when(k > 0)
        def _():
            n_copy(k, src).start()
            s_copy(k, src).start()

        return carry

    lax.fori_loop(0, N_CTX, block, 0)

    own = []
    for kind in range(2):
        stat = jnp.full((tok, HEAD), NEG, F32)
        if kind == 1:
            key = dk_ref[...].astype(F32)
            for h in range(heads):
                query = dq_ref[:, h * HEAD : (h + 1) * HEAD].astype(F32)
                score = jnp.sum(query * key, -1, keepdims=True)
                stat = jnp.where(lane == h, score, stat)
        own.append(stat)
    own_top = jnp.concatenate(own, 0).T[:8]

    def finish(k, carry):
        q_copy(k).wait_send()
        n_copy(k, ahead(k)).wait()
        s_copy(k, ahead(k)).wait()
        return carry

    lax.fori_loop(1, N_CTX, finish, 0)
    stat_in[0] = stat_out[0]
    num_in[0] = num_out[0]
    total = own_top
    for k in range(N_CTX):
        total = jnp.maximum(total, stat_in[k, :8])
    own_weight = jnp.exp2((own_top - total) * SCALE2)
    denom = own_weight
    weights = []
    for k in range(N_CTX):
        w = jnp.exp2((stat_in[k, :8] - total) * SCALE2)
        denom = denom + w * stat_in[k, 8:16]
        weights.append(w)
    weights = (jnp.concatenate(weights, 0) / jnp.concatenate([denom] * N_CTX, 0)).T
    own_weight = jnp.concatenate([own_weight / denom] * N_CTX, 0).T
    for h in range(heads):
        columns = slice(h * HEAD, (h + 1) * HEAD)
        acc = jnp.zeros((2 * tok, HEAD), F32)
        for k in range(N_CTX):
            acc = acc + weights[:, k * 8 + h : k * 8 + h + 1] * num_in[k, :, columns].astype(F32)
        own_value = own_weight[tok:, h : h + 1] * dv_ref[...].astype(F32)
        attn_ref[:tok, columns] = acc[:tok].astype(BF16)
        attn_ref[tok:, columns] = (acc[tok:] + own_value).astype(BF16)


def expert_kernel(
    attn_ref, sr_ref, dr_ref, gain_ref, router_ref, se_ref, de_ref,
    ow_hbm, wg_hbm, wu_hbm, wd_hbm,
    span_ref, dec_ref,
    ow, wg, wu, wd, cout, cin, xout, xin, stream_ref, norm_ref, mout, min_, xg, hid, po,
    r1, r2, ph, r3, r4, fin, rout, rin,
    w_sem, c_send, c_recv, x_send, x_recv, a_send, a_recv, g_send, g_recv,
    r_send, r_recv, b_send, b_recv,
):
    quarter = xg.shape[-1]
    me_c, me_e = lax.axis_index("ctx"), lax.axis_index("exp")
    my_y, my_z = me_c // NZ, me_c % NZ
    my_x, my_k = me_e // 2, me_e % 2
    tok = attn_ref.shape[0] // 2
    rows = tok // N_EXP
    slots = 4 * N_EXP

    def along(axis, step):
        if axis == 0:
            return ((my_y + step) % NY) * NZ + my_z
        return my_y * NZ + (my_z + step) % NZ

    def load(i, src, dst):
        return pltpu.make_async_copy(src, dst, w_sem.at[i])

    loads = [load(q, ow_hbm.at[:, pl.ds(q * quarter, quarter)], ow.at[q]) for q in range(4)]
    loads += [load(4, wg_hbm.at[0], wg), load(5, wu_hbm.at[0], wu)]
    loads += [load(6 + q, wd_hbm.at[0, :, pl.ds(q * quarter, quarter)], wd.at[q]) for q in range(4)]
    for c in loads:
        c.start()

    barrier = pltpu.get_barrier_semaphore()
    for k in range(1, N_EXP):
        pl.semaphore_signal(
            barrier, inc=1, device_id={"exp": (me_e + k) % N_EXP}, device_id_type=MESH
        )
    for axis in range(2):
        for step in (1, 3):
            pl.semaphore_signal(
                barrier, inc=1, device_id={"ctx": along(axis, step)}, device_id_type=MESH
            )
    pl.semaphore_wait(barrier, N_EXP - 1 + 4)

    other = me_e + 1 - 2 * my_k

    def c_copy(q):
        return copy_to(cout.at[q], cin.at[q], c_send.at[q], c_recv.at[q], exp=other)

    def x_copy(q, step):
        return copy_to(
            xout.at[q, (my_x + step) % N_X], xin.at[q, step - 1],
            x_send.at[q * 3 + step - 1], x_recv.at[q * 3 + step - 1],
            exp=((my_x + step) % N_X) * 2 + my_k,
        )

    for q in range(4):
        loads[q].wait()
        part = jnp.dot(attn_ref[...], ow[q], preferred_element_type=F32)
        for e in range(N_EXP):
            both = jnp.concatenate(
                [part[e * rows : (e + 1) * rows], part[tok + e * rows : tok + (e + 1) * rows]], 0
            )

            @pl.when(my_k == e % 2)
            def _():
                xout[q, e // 2] = both.astype(BF16)

            @pl.when(my_k != e % 2)
            def _():
                cout[q, e // 2] = both.astype(BF16)

        c_copy(q).start()
    for q in range(4):
        c_copy(q).wait_recv()
        xout[q] = (xout[q].astype(F32) + cin[q].astype(F32)).astype(BF16)
        for step in (1, 3, 2):
            x_copy(q, step).start()
    for q in range(4):
        columns = slice(q * quarter, (q + 1) * quarter)
        total = xout[q, my_x].astype(F32)
        for step in (1, 2, 3):
            x_copy(q, step).wait_recv()
            total = total + xin[q, step - 1].astype(F32)
        resid = jnp.concatenate(
            [sr_ref[:, columns].astype(F32), dr_ref[:, columns].astype(F32)], 0
        )
        stream_ref[:, columns] = total + resid

    width = 4 * quarter
    square = jnp.zeros((2 * rows, 1), F32)
    for q in range(4):
        part = stream_ref[:, q * quarter : (q + 1) * quarter]
        square = square + jnp.sum(part * part, -1, keepdims=True)
    inverse = lax.rsqrt(square / width + EPS)
    logits = jnp.zeros((2 * rows, router_ref.shape[1]), F32)
    for q in range(4):
        columns = slice(q * quarter, (q + 1) * quarter)
        normed = (stream_ref[:, columns] * inverse * gain_ref[:, columns].astype(F32)).astype(BF16)
        norm_ref[:, columns] = normed
        logits = logits + jnp.dot(normed, router_ref[columns], preferred_element_type=F32)
    ids = jnp.concatenate([se_ref[...], de_ref[...]], 0)
    e_lane = lax.broadcasted_iota(jnp.int32, logits.shape, 1)
    chosen = ids == e_lane
    gate = jax.nn.sigmoid(jnp.sum(jnp.where(chosen, logits, 0.0), -1, keepdims=True))
    row_a = lax.broadcasted_iota(jnp.int32, (2 * rows, 2 * rows), 0)
    row_b = lax.broadcasted_iota(jnp.int32, (2 * rows, 2 * rows), 1)
    earlier = (row_b < row_a) & ((row_b < rows) == (row_a < rows))
    chosen_f = jnp.where(chosen, 1.0, 0.0)
    counts = jnp.dot(
        jnp.where(earlier, 1.0, 0.0).astype(BF16), chosen_f.astype(BF16),
        preferred_element_type=F32,
    )
    slot = jnp.sum(chosen_f * counts, -1, keepdims=True)
    kind = jnp.where(lax.broadcasted_iota(jnp.int32, (2 * rows, 1), 0) < rows, 0.0, 2.0)
    place = ids.astype(F32) * 16.0 + kind + slot
    place = jnp.concatenate([place + 4.0 * q for q in range(4)], 0)
    m_lane = lax.broadcasted_iota(jnp.int32, (8 * rows, 4 * slots), 1).astype(F32)
    pick = jnp.where(place == m_lane, 1.0, 0.0).astype(BF16)
    routed = jnp.concatenate(
        [
            (norm_ref[:, q * quarter : (q + 1) * quarter].astype(F32) * gate).astype(BF16)
            for q in range(4)
        ],
        0,
    )
    sent = lax.dot_general(
        pick, routed, (((0,), (0,)), ((), ())), preferred_element_type=F32
    ).astype(BF16)
    for e in range(N_EXP):
        mout[e] = sent[e * 16 : (e + 1) * 16]

    def a_copy(k):
        dst = (me_e + k) % N_EXP
        return copy_to(mout.at[dst], min_.at[me_e], a_send.at[k], a_recv.at[k], exp=dst)

    for k in range(1, N_EXP):
        a_copy(k).start()
    min_[me_e] = mout[me_e]
    for k in range(1, N_EXP):
        a_copy(k).wait_recv()

    to_row = lax.broadcasted_iota(jnp.int32, (4 * slots, 4 * slots), 0)
    from_row = lax.broadcasted_iota(jnp.int32, (4 * slots, 4 * slots), 1)
    wanted = (to_row % slots) // 4 * 16 + (to_row // slots) * 4 + to_row % 4
    perm = jnp.where(wanted == from_row, 1.0, 0.0).astype(BF16)
    wanted_back = (to_row % 16) // 4 * slots + (to_row // 16) * 4 + to_row % 4
    perm_back = jnp.where(wanted_back == from_row, 1.0, 0.0).astype(BF16)
    arrived = min_[...].reshape(4 * slots, quarter)
    arrived = jnp.dot(perm, arrived, preferred_element_type=F32).astype(BF16)
    for q in range(4):
        xg[q, my_y, my_z] = arrived[q * slots : (q + 1) * slots]

    def g_block(half, phase, line, step):
        first = 1 - half
        axis = first if phase == 0 else 1 - first
        base = [my_y, my_z]
        if phase == 1:
            base[first] = (base[first] + line) % 4
        base[axis] = (base[axis] + step) % 4
        return axis, base[0], base[1]

    def g_copy(half, phase, line, direction, piece, hop):
        axis, _, _ = g_block(half, phase, line, 0)
        step = 0 if hop == 0 else (3 if direction == 0 else 1)
        _, by, bz = g_block(half, phase, line, step)
        q = 2 * half + piece
        slot_ = 0 if phase == 0 else 1 + line
        index = (half * 5 + slot_) * 6 + (direction * 2 + piece if hop == 0 else 4 + direction)
        return copy_to(
            xg.at[q, by, bz], xg.at[q, by, bz], g_send.at[index], g_recv.at[index],
            ctx=along(axis, 1 if direction == 0 else 3),
        )

    def g_start(half, phase, line):
        for piece in range(2):
            g_copy(half, phase, line, 0, piece, 0).start()
            g_copy(half, phase, line, 1, 1 - piece, 0).start()

    def g_forward(half, phase, line):
        for direction in range(2):
            g_copy(half, phase, line, direction, direction, 0).wait_recv()
            g_copy(half, phase, line, direction, direction, 1).start()

    def g_near(half, phase, line):
        for direction in range(2):
            g_copy(half, phase, line, direction, 1 - direction, 0).wait_recv()

    def g_far(half, phase, line):
        for direction in range(2):
            g_copy(half, phase, line, direction, direction, 1).wait_recv()

    def g_sent(half, phase, line):
        for direction in range(2):
            for piece in range(2):
                g_copy(half, phase, line, direction, piece, 0).wait_send()
            g_copy(half, phase, line, direction, direction, 1).wait_send()

    for half in range(2):
        g_start(half, 0, 0)
    for half in range(2):
        g_start(half, 1, 0)
    for half in range(2):
        g_forward(half, 0, 0)
    for half in range(2):
        g_near(half, 0, 0)
        g_start(half, 1, 1)
        g_start(half, 1, 3)
    for half in range(2):
        g_forward(half, 1, 0)
    for half in range(2):
        g_far(half, 0, 0)
        g_start(half, 1, 2)
    for line in (1, 3, 2):
        for half in range(2):
            g_forward(half, 1, line)
    for line in range(4):
        for half in range(2):
            g_near(half, 1, line)
            g_far(half, 1, line)

    loads[4].wait()
    loads[5].wait()

    def hidden_rows(i, carry):
        gate_h = jnp.zeros((2 * NZ * slots, wg.shape[1]), F32)
        up_h = jnp.zeros((2 * NZ * slots, wg.shape[1]), F32)
        for q in range(4):
            x = xg[q, pl.ds(2 * i, 2)].reshape(2 * NZ * slots, quarter)
            w_rows = slice(q * quarter, (q + 1) * quarter)
            gate_h = gate_h + jnp.dot(x, wg[w_rows], preferred_element_type=F32)
            up_h = up_h + jnp.dot(x, wu[w_rows], preferred_element_type=F32)
        hid[i] = (gate_h / (1.0 + jnp.exp(-gate_h)) * up_h).astype(BF16)
        return carry

    lax.fori_loop(0, 2, hidden_rows, 0)

    def r_line(ref, q, axis, step):
        if axis == 0:
            return ref.at[q, (my_y + step) % NY]
        return ref.at[q, :, (my_z + step) % NZ]

    def r_copy(half, phase, direction, piece, hop):
        axis = half if phase == 0 else 1 - half
        q = 2 * half + piece
        step = 2 if hop == 0 else (1 if direction == 0 else 3)
        index = (half * 2 + phase) * 6 + (4 + direction if hop == 0 else direction * 2 + piece)
        if phase == 0:
            src = r_line(po, q, axis, step)
            dst = r1.at[half, direction] if hop == 0 else r2.at[half, direction, piece]
        else:
            coord = my_y if axis == 0 else my_z
            src = ph.at[q, (coord + step) % 4]
            dst = r3.at[half, direction] if hop == 0 else r4.at[half, direction, piece]
        return copy_to(
            src, dst, r_send.at[index], r_recv.at[index],
            ctx=along(axis, 1 if direction == 0 else 3),
        )

    def r_begin(half, phase):
        for direction in range(2):
            r_copy(half, phase, direction, direction, 0).start()
        for direction in range(2):
            r_copy(half, phase, direction, 1 - direction, 1).start()

    def r_middle(half, phase):
        axis = half if phase == 0 else 1 - half
        for direction in range(2):
            r_copy(half, phase, direction, direction, 0).wait_recv()
            q = 2 * half + direction
            step = 1 if direction == 0 else 3
            if phase == 0:
                line = r_line(po, q, axis, step)
                line[...] = (line[...].astype(F32) + r1[half, direction].astype(F32)).astype(BF16)
            else:
                coord = ((my_y if axis == 0 else my_z) + step) % 4
                ph[q, coord] = (
                    ph[q, coord].astype(F32) + r3[half, direction].astype(F32)
                ).astype(BF16)
            r_copy(half, phase, direction, direction, 1).start()

    def r_finish(half, phase):
        axis = half if phase == 0 else 1 - half
        for direction in range(2):
            for piece in range(2):
                r_copy(half, phase, direction, piece, 1).wait_recv()
        for piece in range(2):
            q = 2 * half + piece
            if phase == 0:
                total = r_line(po, q, axis, 0)[...].astype(F32)
                total = total + r2[half, 0, piece].astype(F32) + r2[half, 1, piece].astype(F32)
                ph[q] = total.astype(BF16)
            else:
                coord = my_y if axis == 0 else my_z
                total = ph[q, coord].astype(F32)
                total = total + r4[half, 0, piece].astype(F32) + r4[half, 1, piece].astype(F32)
                fin[q] = total.astype(BF16)

    def r_sent(half, phase):
        for direction in range(2):
            r_copy(half, phase, direction, direction, 0).wait_send()
            for piece in range(2):
                r_copy(half, phase, direction, piece, 1).wait_send()

    def down(q):
        loads[6 + q].wait()
        for i in range(2):
            part = jnp.dot(hid[i], wd[q], preferred_element_type=F32)
            po[q, 2 * i : 2 * i + 2] = part.astype(BF16).reshape(2, NZ, slots, quarter)

    down(0)
    down(1)
    r_begin(0, 0)
    down(2)
    down(3)
    r_begin(1, 0)
    for half in range(2):
        r_middle(half, 0)
    for half in range(2):
        r_finish(half, 0)
        r_begin(half, 1)
    for half in range(2):
        r_middle(half, 1)
    for half in range(2):
        r_finish(half, 1)

    back = jnp.dot(
        perm_back, fin[...].reshape(4 * slots, quarter), preferred_element_type=F32
    ).astype(BF16)
    for e in range(N_EXP):
        rout[e] = back[e * 16 : (e + 1) * 16]

    def b_copy(k):
        dst = (me_e + k) % N_EXP
        return copy_to(rout.at[dst], rin.at[me_e], b_send.at[k], b_recv.at[k], exp=dst)

    for k in range(1, N_EXP):
        b_copy(k).start()
    rin[me_e] = rout[me_e]
    for k in range(1, N_EXP):
        b_copy(k).wait_recv()
    result = jnp.dot(pick, rin[...].reshape(4 * slots, quarter), preferred_element_type=F32)
    for q in range(4):
        columns = slice(q * quarter, (q + 1) * quarter)
        both = stream_ref[:, columns] + result[q * 2 * rows : (q + 1) * 2 * rows]
        span_ref[:, columns] = both[:rows].astype(BF16)
        dec_ref[:, columns] = both[rows:].astype(BF16)

    for q in range(4):
        c_copy(q).wait_send()
        for step in (1, 2, 3):
            x_copy(q, step).wait_send()
    for k in range(1, N_EXP):
        a_copy(k).wait_send()
        b_copy(k).wait_send()
    for half in range(2):
        g_sent(half, 0, 0)
        for line in range(4):
            g_sent(half, 1, line)
        for phase in range(2):
            r_sent(half, phase)


def on_device(
    span_q, decode_q, k_cache, v_cache, span_k, span_v, decode_k, decode_v, decode_pos,
    out_weight, span_resid, decode_resid, norm_gain, router, span_expert, decode_expert,
    w_gate, w_up, w_down,
):
    tok, width = span_q.shape
    pre = k_cache.shape[0]
    model = out_weight.shape[1]
    hidden = w_gate.shape[2]
    quarter = model // 4
    rows = tok // N_EXP
    slots = 4 * N_EXP
    vmem = pl.BlockSpec(memory_space=pltpu.VMEM)
    hbm = pl.BlockSpec(memory_space=pl.ANY)
    dma = pltpu.SemaphoreType.DMA
    positions = jnp.broadcast_to(decode_pos.reshape(N_CTX, tok, 1), (N_CTX, tok, HEAD))
    attn = pl.pallas_call(
        attention_kernel,
        out_shape=jax.ShapeDtypeStruct((2 * tok, width), BF16),
        in_specs=[vmem] * 9,
        out_specs=vmem,
        scratch_shapes=[
            pltpu.VMEM((N_CTX, 2 * tok, width), BF16),
            pltpu.VMEM((pre + HEAD, HEAD), BF16),
            pltpu.VMEM((pre + HEAD, 2 * HEAD), BF16),
            pltpu.VMEM((N_CTX, 2 * tok, width), BF16),
            pltpu.VMEM((N_CTX, 16, 2 * tok), F32),
            pltpu.VMEM((N_CTX, 2 * tok, width), BF16),
            pltpu.VMEM((N_CTX, 16, 2 * tok), F32),
        ]
        + [dma((N_CTX,))] * 6,
        compiler_params=pltpu.CompilerParams(
            collective_id=0, has_side_effects=True, vmem_limit_bytes=60 * 2**20
        ),
        name="attention",
    )(
        span_q, decode_q, positions, k_cache, v_cache, span_k, span_v, decode_k, decode_v,
    )
    out = jax.ShapeDtypeStruct((rows, model), BF16)
    span_out, decode_out = pl.pallas_call(
        expert_kernel,
        out_shape=(out, out),
        in_specs=[vmem] * 7 + [hbm] * 4,
        out_specs=(vmem, vmem),
        scratch_shapes=[
            pltpu.VMEM((4, width, quarter), BF16),
            pltpu.VMEM((model, hidden), BF16),
            pltpu.VMEM((model, hidden), BF16),
            pltpu.VMEM((4, hidden, quarter), BF16),
            pltpu.VMEM((4, N_X, 2 * rows, quarter), BF16),
            pltpu.VMEM((4, N_X, 2 * rows, quarter), BF16),
            pltpu.VMEM((4, N_X, 2 * rows, quarter), BF16),
            pltpu.VMEM((4, N_X - 1, 2 * rows, quarter), BF16),
            pltpu.VMEM((2 * rows, model), F32),
            pltpu.VMEM((2 * rows, model), BF16),
            pltpu.VMEM((N_EXP, 16, quarter), BF16),
            pltpu.VMEM((N_EXP, 16, quarter), BF16),
            pltpu.VMEM((4, NY, NZ, slots, quarter), BF16),
            pltpu.VMEM((2, 2 * NZ * slots, hidden), BF16),
            pltpu.VMEM((4, NY, NZ, slots, quarter), BF16),
            pltpu.VMEM((2, 2, 4, slots, quarter), BF16),
            pltpu.VMEM((2, 2, 2, 4, slots, quarter), BF16),
            pltpu.VMEM((4, 4, slots, quarter), BF16),
            pltpu.VMEM((2, 2, slots, quarter), BF16),
            pltpu.VMEM((2, 2, 2, slots, quarter), BF16),
            pltpu.VMEM((4, slots, quarter), BF16),
            pltpu.VMEM((N_EXP, 16, quarter), BF16),
            pltpu.VMEM((N_EXP, 16, quarter), BF16),
            dma((10,)),
            dma((4,)), dma((4,)),
            dma((12,)), dma((12,)),
            dma((N_EXP,)), dma((N_EXP,)),
            dma((60,)), dma((60,)),
            dma((24,)), dma((24,)),
            dma((N_EXP,)), dma((N_EXP,)),
        ],
        compiler_params=pltpu.CompilerParams(
            collective_id=1, has_side_effects=True, vmem_limit_bytes=60 * 2**20
        ),
        name="experts",
    )(
        attn, span_resid, decode_resid, norm_gain.reshape(1, model), router,
        span_expert, decode_expert, out_weight, w_gate, w_up, w_down,
    )
    return span_out, decode_out


def solution(mesh):
    rows = P(("ctx", "exp"), None)
    both = P("ctx", "exp")
    in_specs = (
        (both,) * 8
        + (P(), P("exp", None), rows, rows, P(), P(), rows, rows)
        + (P("exp", None, "ctx"), P("exp", None, "ctx"), P("exp", "ctx", None))
    )
    return jax.shard_map(
        on_device, mesh=mesh, in_specs=in_specs, out_specs=(rows, rows), check_vma=False
    )
```

```python
import functools

import jax
import jax.numpy as jnp
from jax import lax
from jax.experimental import pallas as pl
from jax.experimental.pallas import tpu as pltpu
from jax.sharding import PartitionSpec as P

HEAD = 128
NEG = -1e30
EPS = 1e-05
SCALE2 = HEAD ** (-0.5) * 1.4426950408889634
NY = 4
NZ = 4
N_CTX = NY * NZ
N_X = 4
N_EXP = 2 * N_X
KEY_TILE = 512
MESH = pl.DeviceIdType.MESH
BF16 = jnp.bfloat16
F32 = jnp.float32


def copy_to(src, dst, send_sem, recv_sem, **where):
    return pltpu.make_async_remote_copy(
        src_ref=src,
        dst_ref=dst,
        send_sem=send_sem,
        recv_sem=recv_sem,
        device_id=where,
        device_id_type=MESH,
    )


class Ring:
    def __init__(self, ref, first, here, along, send, recv, base):
        self.ref, self.first, self.here, self.along = ref, first, here, along
        self.send, self.recv, self.base = send, recv, base

    def copy(self, phase, line, direction, piece, hop):
        axis = self.first if phase == 0 else 1 - self.first
        at = list(self.here)
        at[self.first] = (at[self.first] + line) % 4
        step = 0 if hop == 0 else (3 if direction == 0 else 1)
        at[axis] = (at[axis] + step) % 4
        index = self.base + (0 if phase == 0 else 1 + line) * 6
        index = index + (direction * 2 + piece if hop == 0 else 4 + direction)
        block = self.ref(piece, at[0], at[1])
        to = self.along(axis, 1 if direction == 0 else 3)
        return copy_to(block, block, self.send.at[index], self.recv.at[index], ctx=to)

    def start(self, phase, line):
        for piece in range(2):
            self.copy(phase, line, 0, piece, 0).start()
            self.copy(phase, line, 1, 1 - piece, 0).start()

    def forward(self, phase, line):
        for direction in range(2):
            self.copy(phase, line, direction, direction, 0).wait_recv()
            self.copy(phase, line, direction, direction, 1).start()

    def near(self, phase, line):
        for direction in range(2):
            self.copy(phase, line, direction, 1 - direction, 0).wait_recv()

    def far(self, phase, line):
        for direction in range(2):
            self.copy(phase, line, direction, direction, 1).wait_recv()

    def sent(self, phase, line):
        for direction in range(2):
            for piece in range(2):
                self.copy(phase, line, direction, piece, 0).wait_send()
            self.copy(phase, line, direction, direction, 1).wait_send()

    def all_sent(self):
        self.sent(0, 0)
        for line in range(4):
            self.sent(1, line)


def layer_kernel(
    sq_ref, dq_ref, pos_ref, sk_ref, sv_ref, dk_ref, dv_ref, sr_ref, dr_ref, gain_ref,
    router_ref, se_ref, de_ref, k_hbm, v_hbm, ow_hbm, wg_hbm, wu_hbm, wd_hbm,
    span_ref, dec_ref,
    qb, kx, vx, pos_cols, num_out, stat_out, num_in, stat_in, mid_out, mid_stat, last_in,
    last_stat, attn, ow, wg, wu, wd, cout, cin, xout, xin, stream_ref, pick_ref, mout, min_,
    xg, po, r1, r2, ph, r3, r4, fin, rout, rin,
    w_sem, q_send, q_recv, n_send, n_recv, s_send, s_recv, l_send, l_recv, t_send, t_recv,
    c_send, c_recv, x_send, x_recv, a_send, a_recv, g_send, g_recv, r_send, r_recv,
    b_send, b_recv,
):
    me_c, me_e = lax.axis_index("ctx"), lax.axis_index("exp")
    here = (me_c // NZ, me_c % NZ)
    my_y, my_z = here
    my_x, my_k = me_e // 2, me_e % 2
    tok = sq_ref.shape[0]
    heads = sq_ref.shape[1] // HEAD
    pre = k_hbm.shape[0]
    piece_w = xg.shape[-1]
    rows = tok // N_EXP

    def along(axis, step):
        if axis == 0:
            return ((my_y + step) % NY) * NZ + my_z
        return my_y * NZ + (my_z + step) % NZ

    barrier = pltpu.get_barrier_semaphore()
    for k in range(1, N_EXP):
        pl.semaphore_signal(
            barrier, inc=1, device_id={"exp": (me_e + k) % N_EXP}, device_id_type=MESH
        )
    for axis in range(2):
        for step in range(1, 4):
            pl.semaphore_signal(
                barrier, inc=1, device_id={"ctx": along(axis, step)}, device_id_type=MESH
            )

    def load(i, src, dst):
        return pltpu.make_async_copy(src, dst, w_sem.at[i])

    quarter = 2 * piece_w
    loads = [load(0, k_hbm, kx.at[pl.ds(0, pre)])]
    loads += [load(1, v_hbm, vx.at[pl.ds(0, pre), pl.ds(0, HEAD)])]
    loads += [load(2 + q, ow_hbm.at[:, pl.ds(q * quarter, quarter)], ow.at[q]) for q in range(4)]
    loads += [load(6, wg_hbm.at[0], wg), load(7, wu_hbm.at[0], wu)]
    loads += [load(8 + q, wd_hbm.at[0, :, pl.ds(q * quarter, quarter)], wd.at[q]) for q in range(4)]
    for c in loads:
        c.start()

    for kind, ref in enumerate((sq_ref, dq_ref)):
        for piece in range(2):
            half = tok // 2
            qb[kind, my_y, my_z, piece] = ref[piece * half : (piece + 1) * half]
    q_rings = [
        Ring(
            lambda piece, y, z, kind=kind: qb.at[kind, y, z, piece],
            1 - kind, here, along, q_send, q_recv, 30 * kind,
        )
        for kind in range(2)
    ]
    pl.semaphore_wait(barrier, N_EXP - 1 + 6)
    q_rings[0].start(0, 0)
    q_rings[0].start(1, 0)

    extra = kx.shape[0] - pre - tok
    kx[pre : pre + tok] = sk_ref[...]
    kx[pre + tok :] = jnp.zeros((extra, HEAD), BF16)
    vx[pre : pre + tok, :HEAD] = sv_ref[...]
    vx[pre + tok :, :HEAD] = jnp.zeros((extra, HEAD), BF16)
    vx[:, HEAD:] = jnp.ones((vx.shape[0], HEAD), BF16)
    pos_f = pos_ref[...].astype(F32)
    pos_f = jnp.concatenate(
        [pos_f, jnp.zeros((HEAD - pos_f.shape[0], HEAD), F32)], 0
    ).T.astype(jnp.int32)
    for b in range(N_CTX):
        start = (b * tok) % HEAD
        column = (b * tok) // HEAD
        pos_cols[b] = jnp.broadcast_to(
            pos_f[start : start + tok, column : column + 1], (tok, HEAD)
        )
    loads[0].wait()
    loads[1].wait()

    lane = lax.broadcasted_iota(jnp.int32, (tok, HEAD), 1)

    def order(k):
        later = (k + 1) % N_CTX
        group, j = later // 4, later % 4
        j = (j + 3 * ((4 - group) // 4)) % 4
        line = (3 * group + 3 * (group * (group - 1) // 2)) % 4
        step = (3 * j + 3 * (j * (j - 1) // 2)) % 4
        return line, step

    def n_copy(kind, line, step):
        index = kind * 12 + line * 3 + step - 1
        to = along(1 - kind, step)
        return (
            copy_to(
                num_out.at[kind, line, step], num_in.at[kind, line, step - 1],
                n_send.at[index], n_recv.at[index], ctx=to,
            ),
            copy_to(
                stat_out.at[kind, line, step], stat_in.at[kind, line, step - 1],
                s_send.at[index], s_recv.at[index], ctx=to,
            ),
        )

    def l_copy(kind, line):
        index = kind * 3 + line - 1
        to = along(kind, line)
        return (
            copy_to(
                mid_out.at[kind, line - 1], last_in.at[kind, line - 1],
                l_send.at[index], l_recv.at[index], ctx=to,
            ),
            copy_to(
                mid_stat.at[kind, line - 1], last_stat.at[kind, line - 1],
                t_send.at[index], t_recv.at[index], ctx=to,
            ),
        )

    def tile_step(q, lo, hi, mask, state):
        s = lax.dot_general(
            q, kx[lo:hi], (((1,), (1,)), ((), ())), preferred_element_type=F32
        )
        s = mask(s, lo)
        top = jnp.max(s, -1, keepdims=True)
        if state is not None:
            old_top, old = state
            top = jnp.maximum(old_top, top)
        w = jnp.exp2((s - top) * SCALE2).astype(BF16)
        out = jnp.dot(w, vx[lo:hi], preferred_element_type=F32)
        if state is not None:
            out = old * jnp.exp2((old_top - top) * SCALE2) + out
        return top, out

    def attend(kind, k):
        line, step = order(k)
        shift = (line, step) if kind == 0 else (step, line)
        src_y, src_z = (my_y + shift[0]) % NY, (my_z + shift[1]) % NZ
        src = src_y * NZ + src_z
        if kind == 0:
            row = lax.broadcasted_iota(jnp.int32, (tok, 1), 0)
            limit = jnp.clip(src * tok + row - me_c * tok + 1, 0, tok)
        else:
            limit = pos_cols[src][:, :1] - me_c * pre
        q = jnp.concatenate([qb[kind, src_y, src_z, 0], qb[kind, src_y, src_z, 1]], 0)
        q = jnp.concatenate([q[:, h * HEAD : (h + 1) * HEAD] for h in range(heads)], 0)
        limit = jnp.concatenate([limit] * heads, 0)

        def mask(s, lo):
            if kind == 0 and lo + s.shape[1] <= pre:
                return s
            column = lax.broadcasted_iota(jnp.int32, s.shape, 1)
            hidden_from = limit + (pre - lo) if kind == 0 else limit - lo
            return jnp.where(column < hidden_from, s, NEG)

        state = None
        last = kx.shape[0] if kind == 0 else pre
        edges = list(range(0, pre, KEY_TILE)) + [last]
        for lo, hi in zip(edges[:-1], edges[1:]):
            state = tile_step(q, lo, hi, mask, state)
        top, out = state
        num = out[:, :HEAD].astype(BF16)
        stat = jnp.zeros((tok, HEAD), F32)
        for h in range(heads):
            part = slice(h * tok, (h + 1) * tok)
            num_out[kind, line, step, :, h * HEAD : (h + 1) * HEAD] = num[part]
            stat = jnp.where(lane == h, top[part], stat)
            stat = jnp.where(lane == 8 + h, out[part, HEAD:], stat)
        stat = jnp.concatenate([stat, jnp.zeros((HEAD - tok, HEAD), F32)], 0)
        stat_out[kind, line, step] = stat.T[:16]

        @pl.when(step != 0)
        def _():
            for c in n_copy(kind, line, step):
                c.start()

    def merge(parts, own=None):
        top = parts[0][1][:8]
        for _, stat in parts[1:]:
            top = jnp.maximum(top, stat[:8])
        if own is not None:
            top = jnp.maximum(top, own[0])
        weights = [jnp.exp2((stat[:8] - top) * SCALE2) for _, stat in parts]
        denom = weights[0] * parts[0][1][8:]
        for w, (_, stat) in zip(weights[1:], parts[1:]):
            denom = denom + w * stat[8:]
        if own is not None:
            own_w = jnp.exp2((own[0] - top) * SCALE2)
            denom = denom + own_w
            weights = [w / denom for w in weights + [own_w]]
        blank = jnp.zeros((HEAD - 8 * len(weights), HEAD), F32)
        weights = jnp.concatenate(weights + [blank], 0).T
        out = []
        for h in range(heads):
            columns = slice(h * HEAD, (h + 1) * HEAD)
            acc = jnp.zeros((tok, HEAD), F32)
            for i, (num, _) in enumerate(parts):
                acc = acc + weights[:tok, i * 8 + h : i * 8 + h + 1] * num[:, columns].astype(F32)
            if own is not None:
                i = len(parts)
                acc = acc + weights[:tok, i * 8 + h : i * 8 + h + 1] * own[1]
            out.append(acc.astype(BF16))
        return jnp.concatenate(out, 1), jnp.concatenate([top, denom], 0)

    def line_parts(kind, line):
        parts = [(num_out.at[kind, line, 0], stat_out[kind, line, 0])]
        for step in range(1, 4):
            for c in n_copy(kind, line, step):
                c.wait_recv()
            parts.append((num_in.at[kind, line, step - 1], stat_in[kind, line, step - 1]))
        return parts

    def merge_line(kind, line):
        num, stat = merge(line_parts(kind, line))
        mid_out[kind, line - 1] = num
        mid_stat[kind, line - 1] = stat
        for c in l_copy(kind, line):
            c.start()

    def merge_rows(kind):
        parts = line_parts(kind, 0)
        for line in range(1, 4):
            for c in l_copy(kind, line):
                c.wait_recv()
            parts.append((last_in.at[kind, line - 1], last_stat[kind, line - 1]))
        top = jnp.full((8, HEAD), NEG, F32)
        value = jnp.zeros((tok, HEAD), F32)
        if kind == 1:
            key = dk_ref[...].astype(F32)
            value = dv_ref[...].astype(F32)
            stat = jnp.full((tok, HEAD), NEG, F32)
            for h in range(heads):
                query = dq_ref[:, h * HEAD : (h + 1) * HEAD].astype(F32)
                stat = jnp.where(lane == h, jnp.sum(query * key, -1, keepdims=True), stat)
            stat = jnp.concatenate([stat, jnp.full((HEAD - tok, HEAD), NEG, F32)], 0)
            top = stat.T[:8]
        num, _ = merge(parts, (top, value))
        attn[kind] = num

    def c_copy(kind, q):
        i = kind * 4 + q
        return copy_to(
            cout.at[kind, q], cin.at[kind, q], c_send.at[i], c_recv.at[i],
            exp=me_e + 1 - 2 * my_k,
        )

    def x_copy(kind, q, step):
        i = kind * 12 + q * 3 + step - 1
        to = (my_x + step) % N_X
        return copy_to(
            xout.at[kind, q, to], xin.at[kind, q, step - 1], x_send.at[i], x_recv.at[i],
            exp=to * 2 + my_k,
        )

    def project(kind):
        for q in range(4):
            if kind == 0:
                loads[2 + q].wait()
            part = jnp.dot(attn[kind], ow[q], preferred_element_type=F32)
            for e in range(N_EXP):
                own = part[e * rows : (e + 1) * rows]
                own = jnp.concatenate([own[:, :piece_w], own[:, piece_w:]], 0).astype(BF16)

                @pl.when(my_k == e % 2)
                def _():
                    xout[kind, q, e // 2] = own

                @pl.when(my_k != e % 2)
                def _():
                    cout[kind, q, e // 2] = own

            c_copy(kind, q).start()

    def chip_sum(kind):
        for q in range(4):
            c_copy(kind, q).wait_recv()
            xout[kind, q] = (xout[kind, q].astype(F32) + cin[kind, q].astype(F32)).astype(BF16)
            for step in (2, 1, 3):
                x_copy(kind, q, step).start()

    def a_copy(kind, k):
        to = (me_e + k) % N_EXP
        i = kind * N_EXP + k
        return copy_to(
            mout.at[kind, to], min_.at[kind, me_e], a_send.at[i], a_recv.at[i], exp=to
        )

    def b_copy(kind, k):
        to = (me_e + k) % N_EXP
        i = kind * N_EXP + k
        return copy_to(
            rout.at[kind, to], rin.at[kind, me_e], b_send.at[i], b_recv.at[i], exp=to
        )

    def route(kind):
        resid_ref, id_ref = (sr_ref, se_ref) if kind == 0 else (dr_ref, de_ref)
        square = jnp.zeros((rows, 1), F32)
        pieces = []
        for q in range(4):
            total = xout[kind, q, my_x].astype(F32)
            for step in (1, 2, 3):
                x_copy(kind, q, step).wait_recv()
                total = total + xin[kind, q, step - 1].astype(F32)
            for i in range(2):
                columns = slice((2 * q + i) * piece_w, (2 * q + i + 1) * piece_w)
                part = total[i * rows : (i + 1) * rows] + resid_ref[:, columns].astype(F32)
                stream_ref[kind, :, columns] = part
                square = square + jnp.sum(part * part, -1, keepdims=True)
                pieces.append(part)
        inverse = lax.rsqrt(square / (8 * piece_w) + EPS)
        logits = jnp.zeros((rows, N_EXP), F32)
        normed = []
        for i, part in enumerate(pieces):
            columns = slice(i * piece_w, (i + 1) * piece_w)
            part = (part * inverse * gain_ref[:, columns].astype(F32)).astype(BF16)
            normed.append(part)
            logits = logits + lax.dot_general(
                part, router_ref[:, columns], (((1,), (1,)), ((), ())),
                preferred_element_type=F32,
            )
        a = lax.broadcasted_iota(jnp.int32, (rows, N_EXP), 0)
        b = lax.broadcasted_iota(jnp.int32, (rows, N_EXP), 1)
        ids = jnp.sum(jnp.where(a == b, id_ref[...].astype(F32), 0.0), -1, keepdims=True)
        chosen = ids == b.astype(F32)
        gate = jax.nn.sigmoid(jnp.sum(jnp.where(chosen, logits, 0.0), -1, keepdims=True))
        chosen = jnp.where(chosen, 1.0, 0.0)
        counts = jnp.dot(
            jnp.where(b < a, 1.0, 0.0), chosen, preferred_element_type=F32
        )
        slot = jnp.sum(chosen * counts, -1, keepdims=True)
        place = ids * 16.0 + slot
        place = jnp.concatenate([place + 2.0 * i for i in range(8)], 0)
        m_lane = lax.broadcasted_iota(jnp.int32, (8 * rows, 16 * N_EXP), 1).astype(F32)
        pick = jnp.where(place == m_lane, 1.0, 0.0).astype(BF16)
        pick_ref[kind] = pick
        routed = jnp.concatenate([part.astype(F32) * gate for part in normed], 0).astype(BF16)
        sent = lax.dot_general(
            pick, routed, (((0,), (0,)), ((), ())), preferred_element_type=F32
        ).astype(BF16)
        for e in range(N_EXP):
            mout[kind, e] = sent[e * 16 : (e + 1) * 16]
        for k in range(1, N_EXP):
            a_copy(kind, k).start()
        min_[kind, me_e] = mout[kind, me_e]

    def swap():
        n = 16 * N_EXP
        to_row = lax.broadcasted_iota(jnp.int32, (n, n), 0)
        from_row = lax.broadcasted_iota(jnp.int32, (n, n), 1)
        wanted = (to_row % 16) // 2 * 16 + (to_row // 16) * 2 + to_row % 2
        return jnp.where(wanted == from_row, 1.0, 0.0).astype(BF16)

    g_rings = [
        [
            Ring(
                lambda piece, y, z, kind=kind, half=half: xg.at[kind, 2 * half + piece, y, z],
                1 - half, here, along, g_send, g_recv, (kind * 2 + half) * 30,
            )
            for half in range(2)
        ]
        for kind in range(2)
    ]

    def gather_a(kind):
        for k in range(1, N_EXP):
            a_copy(kind, k).wait_recv()
        arrived = min_[kind].reshape(16 * N_EXP, piece_w)
        arrived = jnp.dot(swap(), arrived, preferred_element_type=F32).astype(BF16)
        for i in range(8):
            xg[kind, i // 2, my_y, my_z, i % 2] = arrived[i * 16 : (i + 1) * 16]
        for ring in g_rings[kind]:
            ring.start(0, 0)
        for ring in g_rings[kind]:
            ring.start(1, 0)

    def gather_b(kind):
        for ring in g_rings[kind]:
            ring.forward(0, 0)
        for ring in g_rings[kind]:
            ring.near(0, 0)
            ring.start(1, 1)
            ring.start(1, 3)

    def gather_c(kind):
        for ring in g_rings[kind]:
            ring.forward(1, 0)
        for ring in g_rings[kind]:
            ring.far(0, 0)
            ring.start(1, 2)

    def gather_d(kind):
        for line in (1, 3):
            for ring in g_rings[kind]:
                ring.forward(1, line)

    def gather_e(kind):
        for ring in g_rings[kind]:
            ring.forward(1, 2)

    def r_line(kind, q, axis, step):
        if axis == 0:
            return po.at[kind, q, (my_y + step) % NY]
        return po.at[kind, q, :, (my_z + step) % NZ]

    def r_copy(kind, half, phase, direction, piece, hop):
        axis = half if phase == 0 else 1 - half
        q = 2 * half + piece
        step = 2 if hop == 0 else (1 if direction == 0 else 3)
        index = (kind * 4 + half * 2 + phase) * 6
        index = index + (4 + direction if hop == 0 else direction * 2 + piece)
        if phase == 0:
            src = r_line(kind, q, axis, step)
            dst = r1.at[kind, half, direction] if hop == 0 else r2.at[kind, half, direction, piece]
        else:
            src = ph.at[kind, q, (here[axis] + step) % 4]
            dst = r3.at[kind, half, direction] if hop == 0 else r4.at[kind, half, direction, piece]
        return copy_to(
            src, dst, r_send.at[index], r_recv.at[index],
            ctx=along(axis, 1 if direction == 0 else 3),
        )

    def r_begin(kind, half, phase):
        for direction in range(2):
            r_copy(kind, half, phase, direction, direction, 0).start()
        for direction in range(2):
            r_copy(kind, half, phase, direction, 1 - direction, 1).start()

    def r_middle(kind, half, phase):
        axis = half if phase == 0 else 1 - half
        for direction in range(2):
            r_copy(kind, half, phase, direction, direction, 0).wait_recv()
            q = 2 * half + direction
            step = 1 if direction == 0 else 3
            if phase == 0:
                line, arrived = r_line(kind, q, axis, step), r1.at[kind, half, direction]
            else:
                line, arrived = ph.at[kind, q, (here[axis] + step) % 4], r3.at[kind, half, direction]
            line[...] = (line[...].astype(F32) + arrived[...].astype(F32)).astype(BF16)
            r_copy(kind, half, phase, direction, direction, 1).start()

    def r_finish(kind, half, phase):
        axis = half if phase == 0 else 1 - half
        for direction in range(2):
            for piece in range(2):
                r_copy(kind, half, phase, direction, piece, 1).wait_recv()
        for piece in range(2):
            q = 2 * half + piece
            if phase == 0:
                own, arrived = r_line(kind, q, axis, 0), r2
            else:
                own, arrived = ph.at[kind, q, here[axis]], r4
            total = own[...].astype(F32)
            for direction in range(2):
                total = total + arrived[kind, half, direction, piece].astype(F32)
            if phase == 0:
                ph[kind, q] = total.astype(BF16)
            else:
                fin[kind, q] = total.astype(BF16)

    def experts(kind):
        for line in range(4):
            for ring in g_rings[kind]:
                ring.near(1, line)
                ring.far(1, line)
        if kind == 0:
            loads[6].wait()
            loads[7].wait()
        n = N_CTX * 16
        gate_h = jnp.zeros((n, wg.shape[1]), F32)
        up_h = jnp.zeros((n, wg.shape[1]), F32)
        for q in range(4):
            x = jnp.concatenate(
                [xg[kind, q, :, :, i].reshape(n, piece_w) for i in range(2)], 1
            )
            w_rows = slice(q * quarter, (q + 1) * quarter)
            gate_h = gate_h + jnp.dot(x, wg[w_rows], preferred_element_type=F32)
            up_h = up_h + jnp.dot(x, wu[w_rows], preferred_element_type=F32)
        hidden = (gate_h / (1.0 + jnp.exp(-gate_h)) * up_h).astype(BF16)
        for q in range(4):
            if kind == 0:
                loads[8 + q].wait()
            part = jnp.dot(hidden, wd[q], preferred_element_type=F32).astype(BF16)
            for i in range(2):
                po[kind, q, :, :, i] = part[:, i * piece_w : (i + 1) * piece_w].reshape(
                    NY, NZ, 16, piece_w
                )
            if q % 2 == 1:
                r_begin(kind, q // 2, 0)

    def sums_b(kind):
        for half in range(2):
            r_middle(kind, half, 0)

    def sums_c(kind):
        for half in range(2):
            r_finish(kind, half, 0)
            r_begin(kind, half, 1)

    def sums_d(kind):
        for half in range(2):
            r_middle(kind, half, 1)

    def give_back(kind):
        for half in range(2):
            r_finish(kind, half, 1)
        back = jnp.dot(
            swap(), fin[kind].reshape(16 * N_EXP, piece_w), preferred_element_type=F32
        ).astype(BF16)
        for e in range(N_EXP):
            rout[kind, e] = back[e * 16 : (e + 1) * 16]
        for k in range(1, N_EXP):
            b_copy(kind, k).start()
        rin[kind, me_e] = rout[kind, me_e]

    def write(kind):
        for k in range(1, N_EXP):
            b_copy(kind, k).wait_recv()
        out_ref = span_ref if kind == 0 else dec_ref
        result = jnp.dot(
            pick_ref[kind], rin[kind].reshape(16 * N_EXP, piece_w), preferred_element_type=F32
        )
        for i in range(8):
            columns = slice(i * piece_w, (i + 1) * piece_w)
            part = stream_ref[kind, :, columns] + result[i * rows : (i + 1) * rows]
            out_ref[:, columns] = part.astype(BF16)

    qs, qd = q_rings

    def do(f, *args):
        return lambda: f(*args)

    span_steps = {
        0: [do(qs.forward, 0, 0), do(qs.near, 0, 0), do(qs.start, 1, 1), do(qs.start, 1, 3),
            do(qd.start, 0, 0), do(qd.start, 1, 0)],
        1: [do(qs.forward, 1, 0), do(qs.far, 0, 0), do(qs.start, 1, 2), do(qs.forward, 1, 3)],
        2: [do(qs.forward, 1, 1), do(qs.near, 1, 0), do(qd.forward, 0, 0), do(qd.near, 0, 0),
            do(qd.start, 1, 1), do(qd.start, 1, 3)],
        3: [do(qs.forward, 1, 2), do(qs.near, 1, 3), do(qd.forward, 1, 0), do(qd.far, 0, 0),
            do(qd.start, 1, 2)],
        4: [do(qs.near, 1, 1), do(qd.forward, 1, 3), do(qd.forward, 1, 1)],
        5: [do(qs.near, 1, 2), do(qd.forward, 1, 2)],
        8: [do(merge_line, 0, 3), do(qd.near, 1, 0)],
        9: [do(qd.near, 1, 3)],
        10: [do(qs.far, 1, 0), do(qs.far, 1, 3), do(qd.near, 1, 1)],
        11: [do(qs.far, 1, 1), do(qs.far, 1, 2), do(qd.near, 1, 2)],
        12: [do(merge_line, 0, 1)],
        13: [do(qd.far, 1, 0), do(qd.far, 1, 3)],
        14: [do(qd.far, 1, 1), do(qd.far, 1, 2)],
    }
    dec_steps = {
        0: [do(merge_line, 0, 2)],
        2: [do(merge_rows, 0), do(project, 0)],
        4: [do(chip_sum, 0)],
        7: [do(route, 0)],
        8: [do(merge_line, 1, 3)],
        9: [do(gather_a, 0)],
        10: [do(gather_b, 0)],
        11: [do(gather_c, 0)],
        12: [do(merge_line, 1, 1), do(gather_d, 0)],
        13: [do(gather_e, 0)],
    }
    tail = [
        do(merge_line, 1, 2), do(experts, 0), do(merge_rows, 1), do(project, 1), do(sums_b, 0),
        do(chip_sum, 1), do(sums_c, 0), do(route, 1), do(sums_d, 0), do(gather_a, 1),
        do(give_back, 0), do(gather_b, 1), do(gather_c, 1), do(gather_d, 1), do(write, 0),
        do(gather_e, 1), do(experts, 1), do(sums_b, 1), do(sums_c, 1), do(sums_d, 1),
        do(give_back, 1), do(write, 1),
    ]

    def loop(kind, steps):
        def one(k, carry):
            attend(kind, k)
            for at, actions in steps.items():

                @pl.when(k == at)
                def _():
                    for action in actions:
                        action()

            return carry

        lax.fori_loop(0, N_CTX, one, 0)

    loop(0, span_steps)
    loop(1, dec_steps)
    for action in tail:
        action()

    for kind in range(2):
        q_rings[kind].all_sent()
        for line in range(4):
            for step in range(1, 4):
                for c in n_copy(kind, line, step):
                    c.wait_send()
        for line in range(1, 4):
            for c in l_copy(kind, line):
                c.wait_send()
        for q in range(4):
            c_copy(kind, q).wait_send()
            for step in (1, 2, 3):
                x_copy(kind, q, step).wait_send()
        for k in range(1, N_EXP):
            a_copy(kind, k).wait_send()
            b_copy(kind, k).wait_send()
        for half in range(2):
            g_rings[kind][half].all_sent()
            for phase in range(2):
                for direction in range(2):
                    r_copy(kind, half, phase, direction, direction, 0).wait_send()
                    for piece in range(2):
                        r_copy(kind, half, phase, direction, piece, 1).wait_send()


def on_device(
    span_q, decode_q, k_cache, v_cache, span_k, span_v, decode_k, decode_v, decode_pos,
    out_weight, span_resid, decode_resid, norm_gain, router, span_expert, decode_expert,
    w_gate, w_up, w_down,
):
    tok, width = span_q.shape
    pre = k_cache.shape[0]
    model = out_weight.shape[1]
    hidden = w_gate.shape[2]
    quarter = model // 4
    piece_w = model // 8
    rows = tok // N_EXP
    vmem = pl.BlockSpec(memory_space=pltpu.VMEM)
    hbm = pl.BlockSpec(memory_space=pl.ANY)
    out = jax.ShapeDtypeStruct((rows, model), BF16)
    unit = (2, 16, piece_w)
    sems = [12, 60, 60, 24, 24, 24, 24, 6, 6, 6, 6, 8, 8, 24, 24, 16, 16, 120, 120, 48, 48, 16, 16]
    return pl.pallas_call(
        layer_kernel,
        out_shape=(out, out),
        in_specs=[vmem] * 13 + [hbm] * 6,
        out_specs=(vmem, vmem),
        scratch_shapes=[
            pltpu.VMEM((2, NY, NZ, 2, tok // 2, width), BF16),
            pltpu.VMEM((pre + HEAD, HEAD), BF16),
            pltpu.VMEM((pre + HEAD, 2 * HEAD), BF16),
            pltpu.VMEM((N_CTX, tok, HEAD), jnp.int32),
            pltpu.VMEM((2, 4, 4, tok, width), BF16),
            pltpu.VMEM((2, 4, 4, 16, HEAD), F32),
            pltpu.VMEM((2, 4, 3, tok, width), BF16),
            pltpu.VMEM((2, 4, 3, 16, HEAD), F32),
            pltpu.VMEM((2, 3, tok, width), BF16),
            pltpu.VMEM((2, 3, 16, HEAD), F32),
            pltpu.VMEM((2, 3, tok, width), BF16),
            pltpu.VMEM((2, 3, 16, HEAD), F32),
            pltpu.VMEM((2, tok, width), BF16),
            pltpu.VMEM((4, width, quarter), BF16),
            pltpu.VMEM((model, hidden), BF16),
            pltpu.VMEM((model, hidden), BF16),
            pltpu.VMEM((4, hidden, quarter), BF16),
            pltpu.VMEM((2, 4, N_X, 2 * rows, piece_w), BF16),
            pltpu.VMEM((2, 4, N_X, 2 * rows, piece_w), BF16),
            pltpu.VMEM((2, 4, N_X, 2 * rows, piece_w), BF16),
            pltpu.VMEM((2, 4, N_X - 1, 2 * rows, piece_w), BF16),
            pltpu.VMEM((2, rows, model), F32),
            pltpu.VMEM((2, 8 * rows, 16 * N_EXP), BF16),
            pltpu.VMEM((2, N_EXP, 16, piece_w), BF16),
            pltpu.VMEM((2, N_EXP, 16, piece_w), BF16),
            pltpu.VMEM((2, 4, NY, NZ) + unit, BF16),
            pltpu.VMEM((2, 4, NY, NZ) + unit, BF16),
            pltpu.VMEM((2, 2, 2, 4) + unit, BF16),
            pltpu.VMEM((2, 2, 2, 2, 4) + unit, BF16),
            pltpu.VMEM((2, 4, 4) + unit, BF16),
            pltpu.VMEM((2, 2, 2) + unit, BF16),
            pltpu.VMEM((2, 2, 2, 2) + unit, BF16),
            pltpu.VMEM((2, 4) + unit, BF16),
            pltpu.VMEM((2, N_EXP, 16, piece_w), BF16),
            pltpu.VMEM((2, N_EXP, 16, piece_w), BF16),
        ]
        + [pltpu.SemaphoreType.DMA((n,)) for n in sems],
        compiler_params=pltpu.CompilerParams(
            collective_id=0, has_side_effects=True, vmem_limit_bytes=62 * 2**20
        ),
        name="layer",
    )(
        span_q, decode_q, decode_pos.reshape(-1, HEAD), span_k, span_v, decode_k, decode_v,
        span_resid, decode_resid, norm_gain.reshape(1, model), router.T,
        span_expert.reshape(1, rows), decode_expert.reshape(1, rows),
        k_cache, v_cache, out_weight, w_gate, w_up, w_down,
    )


def solution(mesh):
    rows = P(("ctx", "exp"), None)
    both = P("ctx", "exp")
    in_specs = (
        (both,) * 8
        + (P(), P("exp", None), rows, rows, P(), P(), rows, rows)
        + (P("exp", None, "ctx"), P("exp", None, "ctx"), P("exp", "ctx", None))
    )
    return jax.shard_map(
        on_device, mesh=mesh, in_specs=in_specs, out_specs=(rows, rows), check_vma=False
    )
```

```python
import functools

import jax
import jax.numpy as jnp
from jax import lax
from jax.experimental import pallas as pl
from jax.experimental.pallas import tpu as pltpu
from jax.sharding import PartitionSpec as P

HEAD = 128
NEG = -1e30
EPS = 1e-05
SCALE2 = HEAD ** (-0.5) * 1.4426950408889634
NY = 4
NZ = 4
N_CTX = NY * NZ
N_X = 4
N_EXP = 2 * N_X
KEY_TILE = 512
MESH = pl.DeviceIdType.MESH
BF16 = jnp.bfloat16
F32 = jnp.float32


def copy_to(src, dst, send_sem, recv_sem, **where):
    return pltpu.make_async_remote_copy(
        src_ref=src,
        dst_ref=dst,
        send_sem=send_sem,
        recv_sem=recv_sem,
        device_id=where,
        device_id_type=MESH,
    )


class Gather:
    def __init__(self, ref, first, here, along, send, recv, base):
        self.ref, self.first, self.here, self.along = ref, first, here, along
        self.send, self.recv, self.base = send, recv, base

    def near_copy(self, step):
        block = self.ref(None, *self.here)
        index = self.base + step - 1
        to = self.along(self.first, step)
        return copy_to(block, block, self.send.at[index], self.recv.at[index], ctx=to)

    def copy(self, line, direction, hop):
        axis = 1 - self.first
        at = list(self.here)
        at[self.first] = (at[self.first] + line) % 4
        if hop == 1:
            at[axis] = (at[axis] + (3 if direction == 0 else 1)) % 4
        index = self.base + 3 + line * 4 + hop * 2 + direction
        block = self.ref(None if hop == 0 else direction, at[0], at[1])
        to = self.along(axis, 1 if direction == 0 else 3)
        return copy_to(block, block, self.send.at[index], self.recv.at[index], ctx=to)

    def begin(self):
        for step in (1, 3, 2):
            self.near_copy(step).start()

    def arrived(self, step):
        self.near_copy(step).wait_recv()

    def start(self, line):
        for direction in range(2):
            self.copy(line, direction, 0).start()

    def forward(self, line):
        for direction in range(2):
            self.copy(line, direction, 0).wait_recv()
            self.copy(line, direction, 1).start()

    def far(self, line):
        for direction in range(2):
            self.copy(line, direction, 1).wait_recv()

    def all_sent(self):
        for step in range(1, 4):
            self.near_copy(step).wait_send()
        for line in range(4):
            for direction in range(2):
                for hop in range(2):
                    self.copy(line, direction, hop).wait_send()


def layer_kernel(
    sq_hbm, dq_hbm, k_hbm, v_hbm, sk_hbm, sv_hbm, ow_hbm, wg_hbm, wu_hbm, wd_hbm,
    pos_hbm, dk_hbm, dv_hbm, sr_hbm, dr_hbm, gain_hbm, router_hbm, se_hbm, de_hbm,
    out_ref,
    pos_ref, dk_ref, dv_ref, sr_ref, dr_ref, gain_ref, router_ref, se_ref, de_ref, qb, kx, vx, pos_cols, num_out, stat_out, num_in, stat_in, mid_out, mid_stat, last_in,
    last_stat, attn, ow, wg, wu, wd, cout, cin, xout, xin, stream_ref, pick_ref, mout, min_,
    xg, po, r1, r2, ph, r4, fin, rout, rin,
    w_sem, q_send, q_recv, n_send, n_recv, s_send, s_recv, l_send, l_recv, t_send, t_recv,
    c_send, c_recv, x_send, x_recv, a_send, a_recv, g_send, g_recv, r_send, r_recv,
    b_send, b_recv,
):
    me_c, me_e = lax.axis_index("ctx"), lax.axis_index("exp")
    here = (me_c // NZ, me_c % NZ)
    my_y, my_z = here
    my_x, my_k = me_e // 2, me_e % 2
    tok = sq_hbm.shape[0]
    heads = sq_hbm.shape[1] // HEAD
    pre = k_hbm.shape[0]
    piece_w = xg.shape[-1]
    rows = tok // N_EXP

    def along(axis, step):
        if axis == 0:
            return ((my_y + step) % NY) * NZ + my_z
        return my_y * NZ + (my_z + step) % NZ

    barrier = pltpu.get_barrier_semaphore()
    for k in range(1, N_EXP):
        pl.semaphore_signal(
            barrier, inc=1, device_id={"exp": (me_e + k) % N_EXP}, device_id_type=MESH
        )
    for axis in range(2):
        for step in range(1, 4):
            pl.semaphore_signal(
                barrier, inc=1, device_id={"ctx": along(axis, step)}, device_id_type=MESH
            )

    def load(i, src, dst):
        return pltpu.make_async_copy(src, dst, w_sem.at[i])

    quarter = 2 * piece_w
    loads = [load(0, k_hbm, kx.at[pl.ds(0, pre)])]
    loads += [load(1, v_hbm, vx.at[pl.ds(0, pre), pl.ds(0, HEAD)])]
    early = [load(12, sq_hbm, qb.at[0, my_y, my_z]), load(13, dq_hbm, qb.at[1, my_y, my_z])]
    early += [load(14, sk_hbm, kx.at[pl.ds(pre, tok)])]
    early += [load(15, sv_hbm, vx.at[pl.ds(pre, tok), pl.ds(0, HEAD)])]
    early += [load(16, pos_hbm, pos_ref)]
    late = [
        load(17 + i, src, dst)
        for i, (src, dst) in enumerate(
            [
                (dk_hbm, dk_ref), (dv_hbm, dv_ref), (sr_hbm, sr_ref), (dr_hbm, dr_ref),
                (gain_hbm, gain_ref), (router_hbm, router_ref), (se_hbm, se_ref),
                (de_hbm, de_ref),
            ]
        )
    ]
    loads += [load(2 + q, ow_hbm.at[:, pl.ds(q * quarter, quarter)], ow.at[q]) for q in range(4)]
    loads += [load(6, wg_hbm.at[0], wg), load(7, wu_hbm.at[0], wu)]
    loads += [load(8 + q, wd_hbm.at[0, :, pl.ds(q * quarter, quarter)], wd.at[q]) for q in range(4)]
    for c in early + loads[:2] + late:
        c.start()

    def load_weights(first, last):
        for c in loads[first:last]:
            c.start()

    extra = kx.shape[0] - pre - tok
    kx[pre + tok :] = jnp.zeros((extra, HEAD), BF16)
    vx[pre + tok :, :HEAD] = jnp.zeros((extra, HEAD), BF16)
    vx[:, HEAD:] = jnp.ones((vx.shape[0], HEAD), BF16)
    early[4].wait()
    pos_f = pos_ref[...].astype(F32)
    pos_f = jnp.concatenate(
        [pos_f, jnp.zeros((HEAD - pos_f.shape[0], HEAD), F32)], 0
    ).T.astype(jnp.int32)
    for b in range(N_CTX):
        start = (b * tok) % HEAD
        column = (b * tok) // HEAD
        pos_cols[b] = jnp.broadcast_to(
            pos_f[start : start + tok, column : column + 1], (tok, HEAD)
        )

    def order(kind, k):
        group, j = (k // 4 + kind) % 4, (k + kind) % 4
        line = (3 * group + 3 * (group * (group - 1) // 2)) % 4
        step = (3 * j + 3 * (j * (j - 1) // 2)) % 4
        return line, step

    def query(kind, line, step):
        if line is None:
            block, index, to = qb.at[kind, my_y, my_z], kind * 15 + step - 1, along(1, step)
        else:
            block, index = qb.at[kind, my_y, (my_z + line) % NZ], kind * 15 + 2 + line * 3 + step
            to = along(0, step)
        return copy_to(block, block, q_send.at[index], q_recv.at[index], ctx=to)

    def queries_z(kind):
        for step in (1, 3, 2):
            query(kind, None, step).start()

    def queries_here(kind):
        for step in (1, 3, 2):
            query(kind, None, step).wait_recv()

    def queries_y(kind, lines, steps):
        for step in steps:
            for line in lines:
                query(kind, line, step).start()

    early[0].wait()
    early[1].wait()
    pl.semaphore_wait(barrier, N_EXP - 1 + 6)

    queries_z(0)
    queries_y(0, (0,), (1,))
    for c in early[2:4] + loads[:2] + late:
        c.wait()

    lane = lax.broadcasted_iota(jnp.int32, (tok, HEAD), 1)

    def n_copy(kind, line, step):
        index = kind * 12 + line * 3 + step - 1
        to = along(1 - kind, step)
        return (
            copy_to(
                num_out.at[kind, line, step], num_in.at[kind, line, step - 1],
                n_send.at[index], n_recv.at[index], ctx=to,
            ),
            copy_to(
                stat_out.at[kind, line, step], stat_in.at[kind, line, step - 1],
                s_send.at[index], s_recv.at[index], ctx=to,
            ),
        )

    def l_copy(kind, line):
        index = kind * 3 + line - 1
        to = along(kind, line)
        return (
            copy_to(
                mid_out.at[kind, line - 1], last_in.at[kind, line - 1],
                l_send.at[index], l_recv.at[index], ctx=to,
            ),
            copy_to(
                mid_stat.at[kind, line - 1], last_stat.at[kind, line - 1],
                t_send.at[index], t_recv.at[index], ctx=to,
            ),
        )

    def tile_step(q, lo, hi, mask, state):
        s = lax.dot_general(
            q, kx[lo:hi], (((1,), (1,)), ((), ())), preferred_element_type=F32
        )
        s = mask(s, lo)
        top = jnp.max(s, -1, keepdims=True)
        if state is not None:
            old_top, old = state
            top = jnp.maximum(old_top, top)
        w = jnp.exp2((s - top) * SCALE2).astype(BF16)
        out = jnp.dot(w, vx[lo:hi], preferred_element_type=F32)
        if state is not None:
            out = old * jnp.exp2((old_top - top) * SCALE2) + out
        return top, out

    def attend(kind, k):
        line, step = order(kind, k)
        across, z_line = (line, step) if kind == 0 else (step, line)

        @pl.when(across != 0)
        def _():
            query(kind, z_line, (4 - across) % 4).wait_recv()

        shift = (line, step) if kind == 0 else (step, line)
        src_y, src_z = (my_y + shift[0]) % NY, (my_z + shift[1]) % NZ
        src = src_y * NZ + src_z
        if kind == 0:
            row = lax.broadcasted_iota(jnp.int32, (tok, 1), 0)
            limit = jnp.clip(src * tok + row - me_c * tok + 1, 0, tok)
        else:
            limit = pos_cols[src][:, :1] - me_c * pre
        q = qb[kind, src_y, src_z]
        q = jnp.concatenate([q[:, h * HEAD : (h + 1) * HEAD] for h in range(heads)], 0)
        limit = jnp.concatenate([limit] * heads, 0)

        def mask(s, lo):
            if kind == 0 and lo + s.shape[1] <= pre:
                return s
            column = lax.broadcasted_iota(jnp.int32, s.shape, 1)
            hidden_from = limit + (pre - lo) if kind == 0 else limit - lo
            return jnp.where(column < hidden_from, s, NEG)

        state = None
        last = kx.shape[0] if kind == 0 else pre
        edges = list(range(0, pre, KEY_TILE)) + [last]
        for lo, hi in zip(edges[:-1], edges[1:]):
            state = tile_step(q, lo, hi, mask, state)
        top, out = state
        num = out[:, :HEAD].astype(BF16)
        stat = jnp.zeros((tok, HEAD), F32)
        for h in range(heads):
            part = slice(h * tok, (h + 1) * tok)
            num_out[kind, line, step, :, h * HEAD : (h + 1) * HEAD] = num[part]
            stat = jnp.where(lane == h, top[part], stat)
            stat = jnp.where(lane == 8 + h, out[part, HEAD:], stat)
        stat = jnp.concatenate([stat, jnp.zeros((HEAD - tok, HEAD), F32)], 0)
        stat_out[kind, line, step] = stat.T[:16]

        @pl.when(step != 0)
        def _():
            for c in n_copy(kind, line, step):
                c.start()

    def merge(parts, own=None):
        top = parts[0][1][:8]
        for _, stat in parts[1:]:
            top = jnp.maximum(top, stat[:8])
        if own is not None:
            top = jnp.maximum(top, own[0])
        weights = [jnp.exp2((stat[:8] - top) * SCALE2) for _, stat in parts]
        denom = weights[0] * parts[0][1][8:]
        for w, (_, stat) in zip(weights[1:], parts[1:]):
            denom = denom + w * stat[8:]
        if own is not None:
            own_w = jnp.exp2((own[0] - top) * SCALE2)
            denom = denom + own_w
            weights = [w / denom for w in weights + [own_w]]
        blank = jnp.zeros((HEAD - 8 * len(weights), HEAD), F32)
        weights = jnp.concatenate(weights + [blank], 0).T
        out = []
        for h in range(heads):
            columns = slice(h * HEAD, (h + 1) * HEAD)
            acc = jnp.zeros((tok, HEAD), F32)
            for i, (num, _) in enumerate(parts):
                acc = acc + weights[:tok, i * 8 + h : i * 8 + h + 1] * num[:, columns].astype(F32)
            if own is not None:
                i = len(parts)
                acc = acc + weights[:tok, i * 8 + h : i * 8 + h + 1] * own[1]
            out.append(acc.astype(BF16))
        return jnp.concatenate(out, 1), jnp.concatenate([top, denom], 0)

    def line_parts(kind, line):
        parts = [(num_out.at[kind, line, 0], stat_out[kind, line, 0])]
        for step in range(1, 4):
            for c in n_copy(kind, line, step):
                c.wait_recv()
            parts.append((num_in.at[kind, line, step - 1], stat_in[kind, line, step - 1]))
        return parts

    def merge_line(kind, line):
        num, stat = merge(line_parts(kind, line))
        mid_out[kind, line - 1] = num
        mid_stat[kind, line - 1] = stat
        for c in l_copy(kind, line):
            c.start()

    def merge_rows(kind):
        parts = line_parts(kind, 0)
        for line in range(1, 4):
            for c in l_copy(kind, line):
                c.wait_recv()
            parts.append((last_in.at[kind, line - 1], last_stat[kind, line - 1]))
        top = jnp.full((8, HEAD), NEG, F32)
        value = jnp.zeros((tok, HEAD), F32)
        if kind == 1:
            key = dk_ref[...].astype(F32)
            value = dv_ref[...].astype(F32)
            stat = jnp.full((tok, HEAD), NEG, F32)
            for h in range(heads):
                query = qb[1, my_y, my_z, :, h * HEAD : (h + 1) * HEAD].astype(F32)
                stat = jnp.where(lane == h, jnp.sum(query * key, -1, keepdims=True), stat)
            stat = jnp.concatenate([stat, jnp.full((HEAD - tok, HEAD), NEG, F32)], 0)
            top = stat.T[:8]
        num, _ = merge(parts, (top, value))
        attn[kind] = num

    def c_copy(kind, q):
        i = kind * 4 + q
        return copy_to(
            cout.at[kind, q], cin.at[kind, q], c_send.at[i], c_recv.at[i],
            exp=me_e + 1 - 2 * my_k,
        )

    def x_copy(kind, q, step):
        i = kind * 12 + q * 3 + step - 1
        to = (my_x + step) % N_X
        return copy_to(
            xout.at[kind, q, to], xin.at[kind, q, step - 1], x_send.at[i], x_recv.at[i],
            exp=to * 2 + my_k,
        )

    def project(kind):
        for q in range(4):
            if kind == 0:
                loads[2 + q].wait()
            part = jnp.dot(attn[kind], ow[q], preferred_element_type=F32)
            for e in range(N_EXP):
                own = part[e * rows : (e + 1) * rows]
                own = jnp.concatenate([own[:, :piece_w], own[:, piece_w:]], 0).astype(BF16)

                @pl.when(my_k == e % 2)
                def _():
                    xout[kind, q, e // 2] = own

                @pl.when(my_k != e % 2)
                def _():
                    cout[kind, q, e // 2] = own

            c_copy(kind, q).start()

    def chip_sum(kind):
        for q in range(4):
            c_copy(kind, q).wait_recv()
            xout[kind, q] = (xout[kind, q].astype(F32) + cin[kind, q].astype(F32)).astype(BF16)
            for step in (2, 1, 3):
                x_copy(kind, q, step).start()

    def a_copy(kind, k):
        to = (me_e + k) % N_EXP
        i = kind * N_EXP + k
        return copy_to(
            mout.at[kind, to], min_.at[kind, me_e], a_send.at[i], a_recv.at[i], exp=to
        )

    def b_copy(kind, k):
        to = (me_e + k) % N_EXP
        i = kind * N_EXP + k
        return copy_to(
            rout.at[kind, to], rin.at[kind, me_e], b_send.at[i], b_recv.at[i], exp=to
        )

    def route(kind):
        resid_ref, id_ref = (sr_ref, se_ref) if kind == 0 else (dr_ref, de_ref)
        square = jnp.zeros((rows, 1), F32)
        pieces = []
        for q in range(4):
            total = xout[kind, q, my_x].astype(F32)
            for step in (1, 2, 3):
                x_copy(kind, q, step).wait_recv()
                total = total + xin[kind, q, step - 1].astype(F32)
            for i in range(2):
                columns = slice((2 * q + i) * piece_w, (2 * q + i + 1) * piece_w)
                part = total[i * rows : (i + 1) * rows] + resid_ref[:, columns].astype(F32)
                stream_ref[kind, :, columns] = part
                square = square + jnp.sum(part * part, -1, keepdims=True)
                pieces.append(part)
        inverse = lax.rsqrt(square / (8 * piece_w) + EPS)
        logits = jnp.zeros((rows, N_EXP), F32)
        normed = []
        for i, part in enumerate(pieces):
            columns = slice(i * piece_w, (i + 1) * piece_w)
            part = (part * inverse * gain_ref[columns].astype(F32).reshape(1, piece_w)).astype(BF16)
            normed.append(part)
            logits = logits + lax.dot_general(
                part, router_ref[:, columns], (((1,), (1,)), ((), ())),
                preferred_element_type=F32,
            )
        a = lax.broadcasted_iota(jnp.int32, (rows, N_EXP), 0)
        b = lax.broadcasted_iota(jnp.int32, (rows, N_EXP), 1)
        ids = jnp.sum(jnp.where(a == b, id_ref[...].astype(F32), 0.0), -1, keepdims=True)
        chosen = ids == b.astype(F32)
        gate = jax.nn.sigmoid(jnp.sum(jnp.where(chosen, logits, 0.0), -1, keepdims=True))
        chosen = jnp.where(chosen, 1.0, 0.0)
        counts = jnp.dot(
            jnp.where(b < a, 1.0, 0.0), chosen, preferred_element_type=F32
        )
        slot = jnp.sum(chosen * counts, -1, keepdims=True)
        place = ids * 16.0 + slot
        place = jnp.concatenate([place + 2.0 * i for i in range(8)], 0)
        m_lane = lax.broadcasted_iota(jnp.int32, (8 * rows, 16 * N_EXP), 1).astype(F32)
        pick = jnp.where(place == m_lane, 1.0, 0.0).astype(BF16)
        pick_ref[kind] = pick
        routed = jnp.concatenate([part.astype(F32) * gate for part in normed], 0).astype(BF16)
        sent = lax.dot_general(
            pick, routed, (((0,), (0,)), ((), ())), preferred_element_type=F32
        ).astype(BF16)
        for e in range(N_EXP):
            mout[kind, e] = sent[e * 16 : (e + 1) * 16]
        for k in range(1, N_EXP):
            a_copy(kind, k).start()
        min_[kind, me_e] = mout[kind, me_e]

    def swap():
        n = 16 * N_EXP
        to_row = lax.broadcasted_iota(jnp.int32, (n, n), 0)
        from_row = lax.broadcasted_iota(jnp.int32, (n, n), 1)
        wanted = (to_row % 16) // 2 * 16 + (to_row // 16) * 2 + to_row % 2
        return jnp.where(wanted == from_row, 1.0, 0.0).astype(BF16)

    def x_block(kind, half):
        def block(piece, y, z):
            if piece is None:
                return xg.at[kind, pl.ds(2 * half, 2), y, z]
            return xg.at[kind, 2 * half + piece, y, z]

        return block

    g_rings = [
        [
            Gather(
                x_block(kind, half), 1 - half, here, along, g_send, g_recv,
                (kind * 2 + half) * 19,
            )
            for half in range(2)
        ]
        for kind in range(2)
    ]

    def gather_a(kind):
        for k in range(1, N_EXP):
            a_copy(kind, k).wait_recv()
        arrived = min_[kind].reshape(16 * N_EXP, piece_w)
        arrived = jnp.dot(swap(), arrived, preferred_element_type=F32).astype(BF16)
        for i in range(8):
            xg[kind, i // 2, my_y, my_z, i % 2] = arrived[i * 16 : (i + 1) * 16]
        for ring in g_rings[kind]:
            ring.begin()
        for ring in g_rings[kind]:
            ring.start(0)

    def gather_b(kind):
        for step in (1, 3, 2):
            for ring in g_rings[kind]:
                ring.arrived(step)
                ring.start((4 - step) % 4)

    def gather_c(kind, *lines):
        for line in lines:
            for ring in g_rings[kind]:
                ring.forward(line)

    def r_line(kind, q, axis, step):
        if axis == 0:
            return po.at[kind, q, (my_y + step) % NY]
        return po.at[kind, q, :, (my_z + step) % NZ]

    def r_copy(kind, half, direction, piece, hop):
        q = 2 * half + piece
        step = 2 if hop == 0 else (1 if direction == 0 else 3)
        index = (kind * 2 + half) * 9 + (4 + direction if hop == 0 else direction * 2 + piece)
        dst = r1.at[kind, half, direction] if hop == 0 else r2.at[kind, half, direction, piece]
        return copy_to(
            r_line(kind, q, half, step), dst, r_send.at[index], r_recv.at[index],
            ctx=along(half, 1 if direction == 0 else 3),
        )

    def r_last(kind, half, step):
        index = (kind * 2 + half) * 9 + 5 + step
        axis = 1 - half
        return copy_to(
            ph.at[kind, half, (here[axis] + step) % 4], r4.at[kind, half, step - 1],
            r_send.at[index], r_recv.at[index], ctx=along(axis, step),
        )

    def r_begin(kind, half):
        for direction in range(2):
            r_copy(kind, half, direction, direction, 0).start()
        for direction in range(2):
            r_copy(kind, half, direction, 1 - direction, 1).start()

    def r_middle(kind, half):
        for direction in range(2):
            r_copy(kind, half, direction, direction, 0).wait_recv()
            q = 2 * half + direction
            line = r_line(kind, q, half, 1 if direction == 0 else 3)
            arrived = r1[kind, half, direction].astype(F32)
            line[...] = (line[...].astype(F32) + arrived).astype(BF16)
            r_copy(kind, half, direction, direction, 1).start()

    def r_middle_done(kind, half):
        for direction in range(2):
            for piece in range(2):
                r_copy(kind, half, direction, piece, 1).wait_recv()
        for piece in range(2):
            total = r_line(kind, 2 * half + piece, half, 0)[...].astype(F32)
            for direction in range(2):
                total = total + r2[kind, half, direction, piece].astype(F32)
            ph[kind, half, :, piece] = total.astype(BF16)
        for step in (2, 1, 3):
            r_last(kind, half, step).start()

    def r_finish(kind, half):
        total = ph[kind, half, here[1 - half]].astype(F32)
        for step in (1, 3, 2):
            r_last(kind, half, step).wait_recv()
            total = total + r4[kind, half, step - 1].astype(F32)
        fin[kind, pl.ds(2 * half, 2)] = total.astype(BF16)

    def experts(kind):
        for line in range(4):
            for ring in g_rings[kind]:
                ring.far(line)
        if kind == 0:
            loads[6].wait()
            loads[7].wait()
        n = N_CTX * 16
        gate_h = jnp.zeros((n, wg.shape[1]), F32)
        up_h = jnp.zeros((n, wg.shape[1]), F32)
        for q in range(4):
            x = jnp.concatenate(
                [xg[kind, q, :, :, i].reshape(n, piece_w) for i in range(2)], 1
            )
            w_rows = slice(q * quarter, (q + 1) * quarter)
            gate_h = gate_h + jnp.dot(x, wg[w_rows], preferred_element_type=F32)
            up_h = up_h + jnp.dot(x, wu[w_rows], preferred_element_type=F32)
        hidden = (gate_h / (1.0 + jnp.exp(-gate_h)) * up_h).astype(BF16)
        for q in range(4):
            if kind == 0:
                loads[8 + q].wait()
            part = jnp.dot(hidden, wd[q], preferred_element_type=F32).astype(BF16)
            for i in range(2):
                po[kind, q, :, :, i] = part[:, i * piece_w : (i + 1) * piece_w].reshape(
                    NY, NZ, 16, piece_w
                )
            if q % 2 == 1:
                r_begin(kind, q // 2)

    def sums_b(kind):
        for half in range(2):
            r_middle(kind, half)

    def sums_c(kind):
        for half in range(2):
            r_middle_done(kind, half)

    def give_back(kind):
        for half in range(2):
            r_finish(kind, half)
        back = jnp.dot(
            swap(), fin[kind].reshape(16 * N_EXP, piece_w), preferred_element_type=F32
        ).astype(BF16)
        for e in range(N_EXP):
            rout[kind, e] = back[e * 16 : (e + 1) * 16]
        for k in range(1, N_EXP):
            b_copy(kind, k).start()
        rin[kind, me_e] = rout[kind, me_e]

    def write(kind):
        for k in range(1, N_EXP):
            b_copy(kind, k).wait_recv()
        result = jnp.dot(
            pick_ref[kind], rin[kind].reshape(16 * N_EXP, piece_w), preferred_element_type=F32
        )
        for i in range(8):
            columns = slice(i * piece_w, (i + 1) * piece_w)
            part = stream_ref[kind, :, columns] + result[i * rows : (i + 1) * rows]
            out_ref[kind, :, columns] = part.astype(BF16)

    def do(f, *args):
        return lambda: f(*args)

    span_steps = {
        0: [do(queries_here, 0), do(queries_y, 0, (3, 1, 2), (1,))],
        2: [do(queries_y, 0, (0, 3, 1, 2), (3,))],
        4: [do(load_weights, 2, 6)],
        5: [do(queries_y, 0, (0, 3, 1, 2), (2,))],
        6: [do(queries_z, 1)],
        8: [do(load_weights, 6, 8)],
        9: [do(queries_here, 1), do(queries_y, 1, (3, 1), (1, 3, 2))],
        10: [do(merge_line, 0, 3)],
        12: [do(load_weights, 8, 12)],
        13: [do(queries_y, 1, (2, 0), (1, 3, 2))],
        14: [do(merge_line, 0, 1)],
    }
    dec_steps = {
        1: [do(merge_line, 0, 2)],
        3: [do(merge_rows, 0), do(project, 0)],
        5: [do(chip_sum, 0), do(merge_line, 1, 3)],
        8: [do(route, 0)],
        9: [do(merge_line, 1, 1)],
        11: [do(gather_a, 0)],
        13: [do(merge_line, 1, 2)],
        14: [do(gather_b, 0)],
    }
    tail = [
        do(merge_rows, 1), do(project, 1), do(chip_sum, 1), do(gather_c, 0, 0, 1, 3),
        do(gather_c, 0, 2), do(route, 1), do(experts, 0), do(gather_a, 1), do(sums_b, 0),
        do(gather_b, 1), do(sums_c, 0), do(gather_c, 1, 0, 1, 3), do(gather_c, 1, 2),
        do(experts, 1), do(sums_b, 1), do(give_back, 0),
        do(sums_c, 1), do(give_back, 1), do(write, 0), do(write, 1),
    ]

    def loop(kind, count, steps):
        def one(k, carry):
            attend(kind, k)
            for at, actions in steps.items():

                @pl.when(k == at)
                def _():
                    for action in actions:
                        action()

            return carry

        lax.fori_loop(0, count, one, 0)

    attend(1, N_CTX - 1)
    loop(0, N_CTX, span_steps)
    loop(1, N_CTX - 1, dec_steps)
    for action in tail:
        action()

    for kind in range(2):
        for step in range(1, 4):
            query(kind, None, step).wait_send()
            for line in range(4):
                query(kind, line, step).wait_send()
    for kind in range(2):
        for line in range(4):
            for step in range(1, 4):
                for c in n_copy(kind, line, step):
                    c.wait_send()
        for line in range(1, 4):
            for c in l_copy(kind, line):
                c.wait_send()
        for q in range(4):
            c_copy(kind, q).wait_send()
            for step in (1, 2, 3):
                x_copy(kind, q, step).wait_send()
        for k in range(1, N_EXP):
            a_copy(kind, k).wait_send()
            b_copy(kind, k).wait_send()
        for half in range(2):
            g_rings[kind][half].all_sent()
            for direction in range(2):
                r_copy(kind, half, direction, direction, 0).wait_send()
                for piece in range(2):
                    r_copy(kind, half, direction, piece, 1).wait_send()
            for step in range(1, 4):
                r_last(kind, half, step).wait_send()


def on_device(
    span_q, decode_q, k_cache, v_cache, span_k, span_v, decode_k, decode_v, decode_pos,
    out_weight, span_resid, decode_resid, norm_gain, router, span_expert, decode_expert,
    w_gate, w_up, w_down,
):
    tok, width = span_q.shape
    pre = k_cache.shape[0]
    model = out_weight.shape[1]
    hidden = w_gate.shape[2]
    quarter = model // 4
    piece_w = model // 8
    rows = tok // N_EXP
    vmem = pl.BlockSpec(memory_space=pltpu.VMEM)
    hbm = pl.BlockSpec(memory_space=pl.ANY)
    out = jax.ShapeDtypeStruct((2, rows, model), BF16)
    unit = (2, 16, piece_w)
    sems = [25, 31, 31, 24, 24, 24, 24, 6, 6, 6, 6, 8, 8, 24, 24, 16, 16, 76, 76, 36, 36, 16, 16]
    both = pl.pallas_call(
        layer_kernel,
        out_shape=out,
        in_specs=[hbm] * 19,
        out_specs=vmem,
        scratch_shapes=[
            pltpu.VMEM((N_CTX * tok // HEAD, HEAD), jnp.int32),
            pltpu.VMEM((tok, HEAD), BF16),
            pltpu.VMEM((tok, HEAD), BF16),
            pltpu.VMEM((rows, model), BF16),
            pltpu.VMEM((rows, model), BF16),
            pltpu.VMEM((model,), BF16),
            pltpu.VMEM((N_EXP, model), BF16),
            pltpu.VMEM((1, rows), jnp.int32),
            pltpu.VMEM((1, rows), jnp.int32),
            pltpu.VMEM((2, NY, NZ, tok, width), BF16),
            pltpu.VMEM((pre + HEAD, HEAD), BF16),
            pltpu.VMEM((pre + HEAD, 2 * HEAD), BF16),
            pltpu.VMEM((N_CTX, tok, HEAD), jnp.int32),
            pltpu.VMEM((2, 4, 4, tok, width), BF16),
            pltpu.VMEM((2, 4, 4, 16, HEAD), F32),
            pltpu.VMEM((2, 4, 3, tok, width), BF16),
            pltpu.VMEM((2, 4, 3, 16, HEAD), F32),
            pltpu.VMEM((2, 3, tok, width), BF16),
            pltpu.VMEM((2, 3, 16, HEAD), F32),
            pltpu.VMEM((2, 3, tok, width), BF16),
            pltpu.VMEM((2, 3, 16, HEAD), F32),
            pltpu.VMEM((2, tok, width), BF16),
            pltpu.VMEM((4, width, quarter), BF16),
            pltpu.VMEM((model, hidden), BF16),
            pltpu.VMEM((model, hidden), BF16),
            pltpu.VMEM((4, hidden, quarter), BF16),
            pltpu.VMEM((2, 4, N_X, 2 * rows, piece_w), BF16),
            pltpu.VMEM((2, 4, N_X, 2 * rows, piece_w), BF16),
            pltpu.VMEM((2, 4, N_X, 2 * rows, piece_w), BF16),
            pltpu.VMEM((2, 4, N_X - 1, 2 * rows, piece_w), BF16),
            pltpu.VMEM((2, rows, model), F32),
            pltpu.VMEM((2, 8 * rows, 16 * N_EXP), BF16),
            pltpu.VMEM((2, N_EXP, 16, piece_w), BF16),
            pltpu.VMEM((2, N_EXP, 16, piece_w), BF16),
            pltpu.VMEM((2, 4, NY, NZ) + unit, BF16),
            pltpu.VMEM((2, 4, NY, NZ) + unit, BF16),
            pltpu.VMEM((2, 2, 2, 4) + unit, BF16),
            pltpu.VMEM((2, 2, 2, 2, 4) + unit, BF16),
            pltpu.VMEM((2, 2, 4, 2) + unit, BF16),
            pltpu.VMEM((2, 2, 3, 2) + unit, BF16),
            pltpu.VMEM((2, 4) + unit, BF16),
            pltpu.VMEM((2, N_EXP, 16, piece_w), BF16),
            pltpu.VMEM((2, N_EXP, 16, piece_w), BF16),
        ]
        + [pltpu.SemaphoreType.DMA((n,)) for n in sems],
        compiler_params=pltpu.CompilerParams(
            collective_id=0, has_side_effects=True, vmem_limit_bytes=62 * 2**20
        ),
        name="layer",
    )(
        span_q, decode_q, k_cache, v_cache, span_k, span_v, out_weight, w_gate, w_up, w_down,
        decode_pos.reshape(-1, HEAD), decode_k, decode_v, span_resid, decode_resid,
        norm_gain, router.T, span_expert.reshape(1, rows),
        decode_expert.reshape(1, rows),
    )
    return both[0], both[1]


def solution(mesh):
    rows = P(("ctx", "exp"), None)
    both = P("ctx", "exp")
    in_specs = (
        (both,) * 8
        + (P(), P("exp", None), rows, rows, P(), P(), rows, rows)
        + (P("exp", None, "ctx"), P("exp", None, "ctx"), P("exp", "ctx", None))
    )
    return jax.shard_map(
        on_device, mesh=mesh, in_specs=in_specs, out_specs=(rows, rows), check_vma=False
    )
```

```python
import functools

import jax
import jax.numpy as jnp
from jax import lax
from jax.experimental import pallas as pl
from jax.experimental.pallas import tpu as pltpu
from jax.sharding import PartitionSpec as P

HEAD = 128
NEG = -1e30
EPS = 1e-05
SCALE2 = HEAD ** (-0.5) * 1.4426950408889634
NY = 4
NZ = 4
N_CTX = NY * NZ
N_X = 4
N_EXP = 2 * N_X
KEY_TILE = 512
MESH = pl.DeviceIdType.MESH
BF16 = jnp.bfloat16
F32 = jnp.float32


def copy_to(src, dst, send_sem, recv_sem, **where):
    return pltpu.make_async_remote_copy(
        src_ref=src,
        dst_ref=dst,
        send_sem=send_sem,
        recv_sem=recv_sem,
        device_id=where,
        device_id_type=MESH,
    )


class Gather:
    def __init__(self, ref, first, here, along, send, recv, base):
        self.ref, self.first, self.here, self.along = ref, first, here, along
        self.send, self.recv, self.base = send, recv, base

    def near_copy(self, step):
        block = self.ref(None, *self.here)
        index = self.base + step - 1
        to = self.along(self.first, step)
        return copy_to(block, block, self.send.at[index], self.recv.at[index], ctx=to)

    def copy(self, line, direction, hop):
        axis = 1 - self.first
        at = list(self.here)
        at[self.first] = (at[self.first] + line) % 4
        if hop == 1:
            at[axis] = (at[axis] + (3 if direction == 0 else 1)) % 4
        index = self.base + 3 + line * 4 + hop * 2 + direction
        block = self.ref(None if hop == 0 else direction, at[0], at[1])
        to = self.along(axis, 1 if direction == 0 else 3)
        return copy_to(block, block, self.send.at[index], self.recv.at[index], ctx=to)

    def begin(self):
        for step in (1, 3, 2):
            self.near_copy(step).start()

    def arrived(self, step):
        self.near_copy(step).wait_recv()

    def start(self, line):
        for direction in range(2):
            self.copy(line, direction, 0).start()

    def forward(self, line):
        for direction in range(2):
            self.copy(line, direction, 0).wait_recv()
            self.copy(line, direction, 1).start()

    def far(self, line):
        for direction in range(2):
            self.copy(line, direction, 1).wait_recv()

    def all_sent(self):
        for step in range(1, 4):
            self.near_copy(step).wait_send()
        for line in range(4):
            for direction in range(2):
                for hop in range(2):
                    self.copy(line, direction, hop).wait_send()


def layer_kernel(
    sq_hbm, dq_hbm, k_hbm, v_hbm, sk_hbm, sv_hbm, ow_hbm, wg_hbm, wu_hbm, wd_hbm,
    pos_hbm, dk_hbm, dv_hbm, sr_hbm, dr_hbm, gain_hbm, router_hbm, se_hbm, de_hbm,
    out_ref,
    pos_ref, dk_ref, dv_ref, sr_ref, dr_ref, gain_ref, router_ref, se_ref, de_ref, qb, kx, vx, pos_cols, num_out, stat_out, num_in, stat_in, mid_out, mid_stat, last_in,
    last_stat, attn, ow, wg, wu, wd, cout, cin, xout, xin, stream_ref, pick_ref, mout, min_,
    xg, po, r1, r2, ph, r4, fin, rout, rin,
    w_sem, q_send, q_recv, n_send, n_recv, s_send, s_recv, l_send, l_recv, t_send, t_recv,
    c_send, c_recv, x_send, x_recv, a_send, a_recv, g_send, g_recv, r_send, r_recv,
    b_send, b_recv,
):
    me_c, me_e = lax.axis_index("ctx"), lax.axis_index("exp")
    here = (me_c // NZ, me_c % NZ)
    my_y, my_z = here
    my_x, my_k = me_e // 2, me_e % 2
    tok = sq_hbm.shape[0]
    heads = sq_hbm.shape[1] // HEAD
    pre = k_hbm.shape[0]
    piece_w = xg.shape[-1]
    rows = tok // N_EXP

    def along(axis, step):
        if axis == 0:
            return ((my_y + step) % NY) * NZ + my_z
        return my_y * NZ + (my_z + step) % NZ

    barrier = pltpu.get_barrier_semaphore()
    for k in range(1, N_EXP):
        pl.semaphore_signal(
            barrier, inc=1, device_id={"exp": (me_e + k) % N_EXP}, device_id_type=MESH
        )
    for axis in range(2):
        for step in range(1, 4):
            pl.semaphore_signal(
                barrier, inc=1, device_id={"ctx": along(axis, step)}, device_id_type=MESH
            )

    def load(i, src, dst):
        return pltpu.make_async_copy(src, dst, w_sem.at[i])

    quarter = 2 * piece_w
    loads = [load(0, k_hbm, kx.at[pl.ds(0, pre)])]
    loads += [load(1, v_hbm, vx.at[pl.ds(0, pre), pl.ds(0, HEAD)])]
    early = [load(12, sq_hbm, qb.at[0, my_y, my_z]), load(13, dq_hbm, qb.at[1, my_y, my_z])]
    early += [load(14, sk_hbm, kx.at[pl.ds(pre, tok)])]
    early += [load(15, sv_hbm, vx.at[pl.ds(pre, tok), pl.ds(0, HEAD)])]
    early += [load(16, pos_hbm, pos_ref)]
    late = [
        load(17 + i, src, dst)
        for i, (src, dst) in enumerate(
            [
                (dk_hbm, dk_ref), (dv_hbm, dv_ref), (sr_hbm, sr_ref), (dr_hbm, dr_ref),
                (gain_hbm, gain_ref), (router_hbm, router_ref), (se_hbm, se_ref),
                (de_hbm, de_ref),
            ]
        )
    ]
    loads += [load(2 + q, ow_hbm.at[:, pl.ds(q * quarter, quarter)], ow.at[q]) for q in range(4)]
    loads += [load(6, wg_hbm.at[0], wg), load(7, wu_hbm.at[0], wu)]
    loads += [load(8 + q, wd_hbm.at[0, :, pl.ds(q * quarter, quarter)], wd.at[q]) for q in range(4)]
    for c in early + loads[:2] + late:
        c.start()

    def load_weights(first, last):
        for c in loads[first:last]:
            c.start()

    extra = kx.shape[0] - pre - tok
    kx[pre + tok :] = jnp.zeros((extra, HEAD), BF16)
    vx[pre + tok :, :HEAD] = jnp.zeros((extra, HEAD), BF16)
    vx[:, HEAD:] = jnp.ones((vx.shape[0], HEAD), BF16)
    early[4].wait()
    pos_f = pos_ref[...].astype(F32)
    pos_f = jnp.concatenate(
        [pos_f, jnp.zeros((HEAD - pos_f.shape[0], HEAD), F32)], 0
    ).T.astype(jnp.int32)
    for b in range(N_CTX):
        start = (b * tok) % HEAD
        column = (b * tok) // HEAD
        pos_cols[b] = jnp.broadcast_to(
            pos_f[start : start + tok, column : column + 1], (tok, HEAD)
        )

    def order(kind, k):
        group, j = (k // 4 + kind) % 4, (k + kind) % 4
        line = (3 * group + 3 * (group * (group - 1) // 2)) % 4
        step = (3 * j + 3 * (j * (j - 1) // 2)) % 4
        return line, step

    def query(kind, line, step):
        if line is None:
            block, index, to = qb.at[kind, my_y, my_z], kind * 15 + step - 1, along(1, step)
        else:
            block, index = qb.at[kind, my_y, (my_z + line) % NZ], kind * 15 + 2 + line * 3 + step
            to = along(0, step)
        return copy_to(block, block, q_send.at[index], q_recv.at[index], ctx=to)

    def queries_z(kind):
        for step in (1, 3, 2):
            query(kind, None, step).start()

    def queries_here(kind):
        for step in (1, 3, 2):
            query(kind, None, step).wait_recv()

    def queries_y(kind, lines, steps):
        for step in steps:
            for line in lines:
                query(kind, line, step).start()

    early[0].wait()
    early[1].wait()
    pl.semaphore_wait(barrier, N_EXP - 1 + 6)

    queries_z(0)
    queries_y(0, (0,), (1,))
    for c in early[2:4] + loads[:2] + late:
        c.wait()

    lane = lax.broadcasted_iota(jnp.int32, (tok, HEAD), 1)

    def n_copy(kind, line, step):
        index = kind * 12 + line * 3 + step - 1
        to = along(1 - kind, step)
        return (
            copy_to(
                num_out.at[kind, line, step], num_in.at[kind, line, step - 1],
                n_send.at[index], n_recv.at[index], ctx=to,
            ),
            copy_to(
                stat_out.at[kind, line, step], stat_in.at[kind, line, step - 1],
                s_send.at[index], s_recv.at[index], ctx=to,
            ),
        )

    def l_copy(kind, line):
        index = kind * 3 + line - 1
        to = along(kind, line)
        return (
            copy_to(
                mid_out.at[kind, line - 1], last_in.at[kind, line - 1],
                l_send.at[index], l_recv.at[index], ctx=to,
            ),
            copy_to(
                mid_stat.at[kind, line - 1], last_stat.at[kind, line - 1],
                t_send.at[index], t_recv.at[index], ctx=to,
            ),
        )

    def tile_step(q, lo, hi, mask, state):
        s = lax.dot_general(
            q, kx[lo:hi], (((1,), (1,)), ((), ())), preferred_element_type=F32
        )
        s = mask(s, lo)
        top = jnp.max(s, -1, keepdims=True)
        if state is not None:
            old_top, old = state
            top = jnp.maximum(old_top, top)
        w = jnp.exp2((s - top) * SCALE2).astype(BF16)
        out = jnp.dot(w, vx[lo:hi], preferred_element_type=F32)
        if state is not None:
            out = old * jnp.exp2((old_top - top) * SCALE2) + out
        return top, out

    def attend(kind, k):
        line, step = order(kind, k)
        across, z_line = (line, step) if kind == 0 else (step, line)

        @pl.when(across != 0)
        def _():
            query(kind, z_line, (4 - across) % 4).wait_recv()

        shift = (line, step) if kind == 0 else (step, line)
        src_y, src_z = (my_y + shift[0]) % NY, (my_z + shift[1]) % NZ
        src = src_y * NZ + src_z
        if kind == 0:
            row = lax.broadcasted_iota(jnp.int32, (tok, 1), 0)
            limit = jnp.clip(src * tok + row - me_c * tok + 1, 0, tok)
        else:
            limit = pos_cols[src][:, :1] - me_c * pre
        q = qb[kind, src_y, src_z]
        q = jnp.concatenate([q[:, h * HEAD : (h + 1) * HEAD] for h in range(heads)], 0)
        limit = jnp.concatenate([limit] * heads, 0)

        def mask(s, lo):
            if kind == 0 and lo + s.shape[1] <= pre:
                return s
            if kind == 0:
                cached, s = s[:, : pre - lo], s[:, pre - lo :]
                column = lax.broadcasted_iota(jnp.int32, s.shape, 1)
                return jnp.concatenate([cached, jnp.where(column < limit, s, NEG)], 1)
            column = lax.broadcasted_iota(jnp.int32, s.shape, 1)
            return jnp.where(column < limit - lo, s, NEG)

        state = None
        last = kx.shape[0] if kind == 0 else pre
        edges = list(range(0, pre, KEY_TILE)) + [last]
        for lo, hi in zip(edges[:-1], edges[1:]):
            state = tile_step(q, lo, hi, mask, state)
        top, out = state
        num = out[:, :HEAD].astype(BF16)
        stat = jnp.zeros((tok, HEAD), F32)
        for h in range(heads):
            part = slice(h * tok, (h + 1) * tok)
            num_out[kind, line, step, :, h * HEAD : (h + 1) * HEAD] = num[part]
            stat = jnp.where(lane == h, top[part], stat)
            stat = jnp.where(lane == 8 + h, out[part, HEAD:], stat)
        stat = jnp.concatenate([stat, jnp.zeros((HEAD - tok, HEAD), F32)], 0)
        stat_out[kind, line, step] = stat.T[:16]

        @pl.when(step != 0)
        def _():
            for c in n_copy(kind, line, step):
                c.start()

    def merge(parts, own=None):
        top = parts[0][1][:8]
        for _, stat in parts[1:]:
            top = jnp.maximum(top, stat[:8])
        if own is not None:
            top = jnp.maximum(top, own[0])
        weights = [jnp.exp2((stat[:8] - top) * SCALE2) for _, stat in parts]
        denom = weights[0] * parts[0][1][8:]
        for w, (_, stat) in zip(weights[1:], parts[1:]):
            denom = denom + w * stat[8:]
        if own is not None:
            own_w = jnp.exp2((own[0] - top) * SCALE2)
            denom = denom + own_w
            weights = [w / denom for w in weights + [own_w]]
        blank = jnp.zeros((HEAD - 8 * len(weights), HEAD), F32)
        weights = jnp.concatenate(weights + [blank], 0).T
        out = []
        for h in range(heads):
            columns = slice(h * HEAD, (h + 1) * HEAD)
            acc = jnp.zeros((tok, HEAD), F32)
            for i, (num, _) in enumerate(parts):
                acc = acc + weights[:tok, i * 8 + h : i * 8 + h + 1] * num[:, columns].astype(F32)
            if own is not None:
                i = len(parts)
                acc = acc + weights[:tok, i * 8 + h : i * 8 + h + 1] * own[1]
            out.append(acc.astype(BF16))
        return jnp.concatenate(out, 1), jnp.concatenate([top, denom], 0)

    def line_parts(kind, line):
        parts = [(num_out.at[kind, line, 0], stat_out[kind, line, 0])]
        for step in range(1, 4):
            for c in n_copy(kind, line, step):
                c.wait_recv()
            parts.append((num_in.at[kind, line, step - 1], stat_in[kind, line, step - 1]))
        return parts

    def merge_line(kind, line):
        num, stat = merge(line_parts(kind, line))
        mid_out[kind, line - 1] = num
        mid_stat[kind, line - 1] = stat
        for c in l_copy(kind, line):
            c.start()

    def merge_rows(kind):
        parts = line_parts(kind, 0)
        for line in range(1, 4):
            for c in l_copy(kind, line):
                c.wait_recv()
            parts.append((last_in.at[kind, line - 1], last_stat[kind, line - 1]))
        top = jnp.full((8, HEAD), NEG, F32)
        value = jnp.zeros((tok, HEAD), F32)
        if kind == 1:
            key = dk_ref[...].astype(F32)
            value = dv_ref[...].astype(F32)
            stat = jnp.full((tok, HEAD), NEG, F32)
            for h in range(heads):
                query = qb[1, my_y, my_z, :, h * HEAD : (h + 1) * HEAD].astype(F32)
                stat = jnp.where(lane == h, jnp.sum(query * key, -1, keepdims=True), stat)
            stat = jnp.concatenate([stat, jnp.full((HEAD - tok, HEAD), NEG, F32)], 0)
            top = stat.T[:8]
        num, _ = merge(parts, (top, value))
        attn[kind] = num

    def c_copy(kind, q):
        i = kind * 4 + q
        return copy_to(
            cout.at[kind, q], cin.at[kind, q], c_send.at[i], c_recv.at[i],
            exp=me_e + 1 - 2 * my_k,
        )

    def x_copy(kind, q, step):
        i = kind * 12 + q * 3 + step - 1
        to = (my_x + step) % N_X
        return copy_to(
            xout.at[kind, q, to], xin.at[kind, q, step - 1], x_send.at[i], x_recv.at[i],
            exp=to * 2 + my_k,
        )

    def project(kind):
        for q in range(4):
            if kind == 0:
                loads[2 + q].wait()
            part = jnp.dot(attn[kind], ow[q], preferred_element_type=F32)
            for e in range(N_EXP):
                own = part[e * rows : (e + 1) * rows]
                own = jnp.concatenate([own[:, :piece_w], own[:, piece_w:]], 0).astype(BF16)

                @pl.when(my_k == e % 2)
                def _():
                    xout[kind, q, e // 2] = own

                @pl.when(my_k != e % 2)
                def _():
                    cout[kind, q, e // 2] = own

            c_copy(kind, q).start()

    def chip_sum(kind):
        for q in range(4):
            c_copy(kind, q).wait_recv()
            xout[kind, q] = (xout[kind, q].astype(F32) + cin[kind, q].astype(F32)).astype(BF16)
            for step in (2, 1, 3):
                x_copy(kind, q, step).start()

    def a_copy(kind, k):
        to = (me_e + k) % N_EXP
        i = kind * N_EXP + k
        return copy_to(
            mout.at[kind, to], min_.at[kind, me_e], a_send.at[i], a_recv.at[i], exp=to
        )

    def b_copy(kind, k):
        to = (me_e + k) % N_EXP
        i = kind * N_EXP + k
        return copy_to(
            rout.at[kind, to], rin.at[kind, me_e], b_send.at[i], b_recv.at[i], exp=to
        )

    def route(kind):
        resid_ref, id_ref = (sr_ref, se_ref) if kind == 0 else (dr_ref, de_ref)
        square = jnp.zeros((rows, 1), F32)
        pieces = []
        for q in range(4):
            total = xout[kind, q, my_x].astype(F32)
            for step in (1, 2, 3):
                x_copy(kind, q, step).wait_recv()
                total = total + xin[kind, q, step - 1].astype(F32)
            for i in range(2):
                columns = slice((2 * q + i) * piece_w, (2 * q + i + 1) * piece_w)
                part = total[i * rows : (i + 1) * rows] + resid_ref[:, columns].astype(F32)
                stream_ref[kind, :, columns] = part
                square = square + jnp.sum(part * part, -1, keepdims=True)
                pieces.append(part)
        inverse = lax.rsqrt(square / (8 * piece_w) + EPS)
        logits = jnp.zeros((rows, N_EXP), F32)
        normed = []
        for i, part in enumerate(pieces):
            columns = slice(i * piece_w, (i + 1) * piece_w)
            part = (part * inverse * gain_ref[columns].astype(F32).reshape(1, piece_w)).astype(BF16)
            normed.append(part)
            logits = logits + lax.dot_general(
                part, router_ref[:, columns], (((1,), (1,)), ((), ())),
                preferred_element_type=F32,
            )
        a = lax.broadcasted_iota(jnp.int32, (rows, N_EXP), 0)
        b = lax.broadcasted_iota(jnp.int32, (rows, N_EXP), 1)
        ids = jnp.sum(jnp.where(a == b, id_ref[...].astype(F32), 0.0), -1, keepdims=True)
        chosen = ids == b.astype(F32)
        gate = jax.nn.sigmoid(jnp.sum(jnp.where(chosen, logits, 0.0), -1, keepdims=True))
        chosen = jnp.where(chosen, 1.0, 0.0)
        counts = jnp.dot(
            jnp.where(b < a, 1.0, 0.0), chosen, preferred_element_type=F32
        )
        slot = jnp.sum(chosen * counts, -1, keepdims=True)
        place = ids * 16.0 + slot
        place = jnp.concatenate([place + 2.0 * i for i in range(8)], 0)
        m_lane = lax.broadcasted_iota(jnp.int32, (8 * rows, 16 * N_EXP), 1).astype(F32)
        pick = jnp.where(place == m_lane, 1.0, 0.0).astype(BF16)
        pick_ref[kind] = pick
        routed = jnp.concatenate([part.astype(F32) * gate for part in normed], 0).astype(BF16)
        sent = lax.dot_general(
            pick, routed, (((0,), (0,)), ((), ())), preferred_element_type=F32
        ).astype(BF16)
        for e in range(N_EXP):
            mout[kind, e] = sent[e * 16 : (e + 1) * 16]
        for k in range(1, N_EXP):
            a_copy(kind, k).start()
        min_[kind, me_e] = mout[kind, me_e]

    def swap():
        n = 16 * N_EXP
        to_row = lax.broadcasted_iota(jnp.int32, (n, n), 0)
        from_row = lax.broadcasted_iota(jnp.int32, (n, n), 1)
        wanted = (to_row % 16) // 2 * 16 + (to_row // 16) * 2 + to_row % 2
        return jnp.where(wanted == from_row, 1.0, 0.0).astype(BF16)

    def x_block(kind, half):
        def block(piece, y, z):
            if piece is None:
                return xg.at[kind, pl.ds(2 * half, 2), y, z]
            return xg.at[kind, 2 * half + piece, y, z]

        return block

    g_rings = [
        [
            Gather(
                x_block(kind, half), 1 - half, here, along, g_send, g_recv,
                (kind * 2 + half) * 19,
            )
            for half in range(2)
        ]
        for kind in range(2)
    ]

    def gather_a(kind):
        for k in range(1, N_EXP):
            a_copy(kind, k).wait_recv()
        arrived = min_[kind].reshape(16 * N_EXP, piece_w)
        arrived = jnp.dot(swap(), arrived, preferred_element_type=F32).astype(BF16)
        for i in range(8):
            xg[kind, i // 2, my_y, my_z, i % 2] = arrived[i * 16 : (i + 1) * 16]
        for ring in g_rings[kind]:
            ring.begin()
        for ring in g_rings[kind]:
            ring.start(0)

    def gather_b(kind):
        for step in (1, 3, 2):
            for ring in g_rings[kind]:
                ring.arrived(step)
                ring.start((4 - step) % 4)

    def gather_c(kind, *lines):
        for line in lines:
            for ring in g_rings[kind]:
                ring.forward(line)

    def r_line(kind, q, axis, step):
        if axis == 0:
            return po.at[kind, q, (my_y + step) % NY]
        return po.at[kind, q, :, (my_z + step) % NZ]

    def r_copy(kind, half, direction, piece, hop):
        q = 2 * half + piece
        step = 2 if hop == 0 else (1 if direction == 0 else 3)
        index = (kind * 2 + half) * 9 + (4 + direction if hop == 0 else direction * 2 + piece)
        dst = r1.at[kind, half, direction] if hop == 0 else r2.at[kind, half, direction, piece]
        return copy_to(
            r_line(kind, q, half, step), dst, r_send.at[index], r_recv.at[index],
            ctx=along(half, 1 if direction == 0 else 3),
        )

    def r_last(kind, half, step):
        index = (kind * 2 + half) * 9 + 5 + step
        axis = 1 - half
        return copy_to(
            ph.at[kind, half, (here[axis] + step) % 4], r4.at[kind, half, step - 1],
            r_send.at[index], r_recv.at[index], ctx=along(axis, step),
        )

    def r_begin(kind, half):
        for direction in range(2):
            r_copy(kind, half, direction, direction, 0).start()
        for direction in range(2):
            r_copy(kind, half, direction, 1 - direction, 1).start()

    def r_middle(kind, half):
        for direction in range(2):
            r_copy(kind, half, direction, direction, 0).wait_recv()
            q = 2 * half + direction
            line = r_line(kind, q, half, 1 if direction == 0 else 3)
            arrived = r1[kind, half, direction].astype(F32)
            line[...] = (line[...].astype(F32) + arrived).astype(BF16)
            r_copy(kind, half, direction, direction, 1).start()

    def r_middle_done(kind, half):
        for direction in range(2):
            for piece in range(2):
                r_copy(kind, half, direction, piece, 1).wait_recv()
        for piece in range(2):
            total = r_line(kind, 2 * half + piece, half, 0)[...].astype(F32)
            for direction in range(2):
                total = total + r2[kind, half, direction, piece].astype(F32)
            ph[kind, half, :, piece] = total.astype(BF16)
        for step in (2, 1, 3):
            r_last(kind, half, step).start()

    def r_finish(kind, half):
        total = ph[kind, half, here[1 - half]].astype(F32)
        for step in (1, 3, 2):
            r_last(kind, half, step).wait_recv()
            total = total + r4[kind, half, step - 1].astype(F32)
        fin[kind, pl.ds(2 * half, 2)] = total.astype(BF16)

    def experts(kind):
        for line in range(4):
            for ring in g_rings[kind]:
                ring.far(line)
        if kind == 0:
            loads[6].wait()
            loads[7].wait()
        n = N_CTX * 16
        gate_h = jnp.zeros((n, wg.shape[1]), F32)
        up_h = jnp.zeros((n, wg.shape[1]), F32)
        for q in range(4):
            x = jnp.concatenate(
                [xg[kind, q, :, :, i].reshape(n, piece_w) for i in range(2)], 1
            )
            w_rows = slice(q * quarter, (q + 1) * quarter)
            gate_h = gate_h + jnp.dot(x, wg[w_rows], preferred_element_type=F32)
            up_h = up_h + jnp.dot(x, wu[w_rows], preferred_element_type=F32)
        hidden = (gate_h / (1.0 + jnp.exp(-gate_h)) * up_h).astype(BF16)
        for q in range(4):
            if kind == 0:
                loads[8 + q].wait()
            part = jnp.dot(hidden, wd[q], preferred_element_type=F32).astype(BF16)
            for i in range(2):
                po[kind, q, :, :, i] = part[:, i * piece_w : (i + 1) * piece_w].reshape(
                    NY, NZ, 16, piece_w
                )
            if q % 2 == 1:
                r_begin(kind, q // 2)

    def sums_b(kind):
        for half in range(2):
            r_middle(kind, half)

    def sums_c(kind):
        for half in range(2):
            r_middle_done(kind, half)

    def give_back(kind):
        for half in range(2):
            r_finish(kind, half)
        back = jnp.dot(
            swap(), fin[kind].reshape(16 * N_EXP, piece_w), preferred_element_type=F32
        ).astype(BF16)
        for e in range(N_EXP):
            rout[kind, e] = back[e * 16 : (e + 1) * 16]
        for k in range(1, N_EXP):
            b_copy(kind, k).start()
        rin[kind, me_e] = rout[kind, me_e]

    def write(kind):
        for k in range(1, N_EXP):
            b_copy(kind, k).wait_recv()
        result = jnp.dot(
            pick_ref[kind], rin[kind].reshape(16 * N_EXP, piece_w), preferred_element_type=F32
        )
        for i in range(8):
            columns = slice(i * piece_w, (i + 1) * piece_w)
            part = stream_ref[kind, :, columns] + result[i * rows : (i + 1) * rows]
            out_ref[kind, :, columns] = part.astype(BF16)

    def do(f, *args):
        return lambda: f(*args)

    span_steps = {
        0: [do(queries_here, 0), do(queries_y, 0, (3, 1, 2), (1,))],
        2: [do(queries_y, 0, (0, 3, 1, 2), (3,))],
        4: [do(load_weights, 2, 6)],
        5: [do(queries_y, 0, (0, 3, 1, 2), (2,))],
        6: [do(queries_z, 1)],
        8: [do(load_weights, 6, 8)],
        9: [do(queries_here, 1), do(queries_y, 1, (3, 1), (1, 3, 2))],
        10: [do(merge_line, 0, 3)],
        12: [do(load_weights, 8, 12)],
        13: [do(queries_y, 1, (2, 0), (1, 3, 2))],
        14: [do(merge_line, 0, 1)],
    }
    dec_steps = {
        1: [do(merge_line, 0, 2)],
        3: [do(merge_rows, 0), do(project, 0)],
        5: [do(chip_sum, 0), do(merge_line, 1, 3)],
        8: [do(route, 0)],
        9: [do(merge_line, 1, 1)],
        11: [do(gather_a, 0)],
        13: [do(merge_line, 1, 2)],
        14: [do(gather_b, 0)],
    }
    tail = [
        do(merge_rows, 1), do(project, 1), do(chip_sum, 1), do(gather_c, 0, 0, 1, 3),
        do(gather_c, 0, 2), do(route, 1), do(experts, 0), do(gather_a, 1), do(sums_b, 0),
        do(gather_b, 1), do(sums_c, 0), do(gather_c, 1, 0, 1, 3), do(gather_c, 1, 2),
        do(experts, 1), do(sums_b, 1), do(give_back, 0),
        do(sums_c, 1), do(give_back, 1), do(write, 0), do(write, 1),
    ]

    def loop(kind, count, steps):
        def one(k, carry):
            attend(kind, k)
            for at, actions in steps.items():

                @pl.when(k == at)
                def _():
                    for action in actions:
                        action()

            return carry

        lax.fori_loop(0, count, one, 0)

    attend(1, N_CTX - 1)
    loop(0, N_CTX, span_steps)
    loop(1, N_CTX - 1, dec_steps)
    for action in tail:
        action()

    for kind in range(2):
        for step in range(1, 4):
            query(kind, None, step).wait_send()
            for line in range(4):
                query(kind, line, step).wait_send()
    for kind in range(2):
        for line in range(4):
            for step in range(1, 4):
                for c in n_copy(kind, line, step):
                    c.wait_send()
        for line in range(1, 4):
            for c in l_copy(kind, line):
                c.wait_send()
        for q in range(4):
            c_copy(kind, q).wait_send()
            for step in (1, 2, 3):
                x_copy(kind, q, step).wait_send()
        for k in range(1, N_EXP):
            a_copy(kind, k).wait_send()
            b_copy(kind, k).wait_send()
        for half in range(2):
            g_rings[kind][half].all_sent()
            for direction in range(2):
                r_copy(kind, half, direction, direction, 0).wait_send()
                for piece in range(2):
                    r_copy(kind, half, direction, piece, 1).wait_send()
            for step in range(1, 4):
                r_last(kind, half, step).wait_send()


def on_device(
    span_q, decode_q, k_cache, v_cache, span_k, span_v, decode_k, decode_v, decode_pos,
    out_weight, span_resid, decode_resid, norm_gain, router, span_expert, decode_expert,
    w_gate, w_up, w_down,
):
    tok, width = span_q.shape
    pre = k_cache.shape[0]
    model = out_weight.shape[1]
    hidden = w_gate.shape[2]
    quarter = model // 4
    piece_w = model // 8
    rows = tok // N_EXP
    vmem = pl.BlockSpec(memory_space=pltpu.VMEM)
    hbm = pl.BlockSpec(memory_space=pl.ANY)
    out = jax.ShapeDtypeStruct((2, rows, model), BF16)
    unit = (2, 16, piece_w)
    sems = [25, 31, 31, 24, 24, 24, 24, 6, 6, 6, 6, 8, 8, 24, 24, 16, 16, 76, 76, 36, 36, 16, 16]
    both = pl.pallas_call(
        layer_kernel,
        out_shape=out,
        in_specs=[hbm] * 19,
        out_specs=vmem,
        scratch_shapes=[
            pltpu.VMEM((N_CTX * tok // HEAD, HEAD), jnp.int32),
            pltpu.VMEM((tok, HEAD), BF16),
            pltpu.VMEM((tok, HEAD), BF16),
            pltpu.VMEM((rows, model), BF16),
            pltpu.VMEM((rows, model), BF16),
            pltpu.VMEM((model,), BF16),
            pltpu.VMEM((N_EXP, model), BF16),
            pltpu.VMEM((1, rows), jnp.int32),
            pltpu.VMEM((1, rows), jnp.int32),
            pltpu.VMEM((2, NY, NZ, tok, width), BF16),
            pltpu.VMEM((pre + HEAD, HEAD), BF16),
            pltpu.VMEM((pre + HEAD, 2 * HEAD), BF16),
            pltpu.VMEM((N_CTX, tok, HEAD), jnp.int32),
            pltpu.VMEM((2, 4, 4, tok, width), BF16),
            pltpu.VMEM((2, 4, 4, 16, HEAD), F32),
            pltpu.VMEM((2, 4, 3, tok, width), BF16),
            pltpu.VMEM((2, 4, 3, 16, HEAD), F32),
            pltpu.VMEM((2, 3, tok, width), BF16),
            pltpu.VMEM((2, 3, 16, HEAD), F32),
            pltpu.VMEM((2, 3, tok, width), BF16),
            pltpu.VMEM((2, 3, 16, HEAD), F32),
            pltpu.VMEM((2, tok, width), BF16),
            pltpu.VMEM((4, width, quarter), BF16),
            pltpu.VMEM((model, hidden), BF16),
            pltpu.VMEM((model, hidden), BF16),
            pltpu.VMEM((4, hidden, quarter), BF16),
            pltpu.VMEM((2, 4, N_X, 2 * rows, piece_w), BF16),
            pltpu.VMEM((2, 4, N_X, 2 * rows, piece_w), BF16),
            pltpu.VMEM((2, 4, N_X, 2 * rows, piece_w), BF16),
            pltpu.VMEM((2, 4, N_X - 1, 2 * rows, piece_w), BF16),
            pltpu.VMEM((2, rows, model), F32),
            pltpu.VMEM((2, 8 * rows, 16 * N_EXP), BF16),
            pltpu.VMEM((2, N_EXP, 16, piece_w), BF16),
            pltpu.VMEM((2, N_EXP, 16, piece_w), BF16),
            pltpu.VMEM((2, 4, NY, NZ) + unit, BF16),
            pltpu.VMEM((2, 4, NY, NZ) + unit, BF16),
            pltpu.VMEM((2, 2, 2, 4) + unit, BF16),
            pltpu.VMEM((2, 2, 2, 2, 4) + unit, BF16),
            pltpu.VMEM((2, 2, 4, 2) + unit, BF16),
            pltpu.VMEM((2, 2, 3, 2) + unit, BF16),
            pltpu.VMEM((2, 4) + unit, BF16),
            pltpu.VMEM((2, N_EXP, 16, piece_w), BF16),
            pltpu.VMEM((2, N_EXP, 16, piece_w), BF16),
        ]
        + [pltpu.SemaphoreType.DMA((n,)) for n in sems],
        compiler_params=pltpu.CompilerParams(
            collective_id=0, has_side_effects=True, vmem_limit_bytes=62 * 2**20
        ),
        name="layer",
    )(
        span_q, decode_q, k_cache, v_cache, span_k, span_v, out_weight, w_gate, w_up, w_down,
        decode_pos.reshape(-1, HEAD), decode_k, decode_v, span_resid, decode_resid,
        norm_gain, router.T, span_expert.reshape(1, rows),
        decode_expert.reshape(1, rows),
    )
    return both[0], both[1]


def solution(mesh):
    rows = P(("ctx", "exp"), None)
    both = P("ctx", "exp")
    in_specs = (
        (both,) * 8
        + (P(), P("exp", None), rows, rows, P(), P(), rows, rows)
        + (P("exp", None, "ctx"), P("exp", None, "ctx"), P("exp", "ctx", None))
    )
    return jax.shard_map(
        on_device, mesh=mesh, in_specs=in_specs, out_specs=(rows, rows), check_vma=False
    )
```
